512 devices in a mesh: row: 16 (over x_hi, y), col: 32 (over z, x_lo, core).
Axes of the slice: x: 4 (x_hi: 2, x_lo: 2; x = x_hi * 2 + x_lo), y: 8, z: 8, core: 2. Of those that a mesh axis runs over, the one named last changes fastest.
Arguments:
- vectors: bfloat16 [512, 32768], P('row', 'col'), may hold values from -6 to 6
- factor_tiles: bfloat16 [128, 96, 256, 256], P('row', 'col'), may hold values from -0.0546875 to 0.0546875
- tile_columns: int32 [128, 96], P('row', 'col'), may hold values from 0 to 127, as said below
- live_counts: int32 [128, 32], P('row', 'col'), may hold values from 0 to 3, as said below
Outputs:
- applied: float32 [512, 32768], P('row', 'col')
The draws below stay inside these ranges and needn't reach their ends.
Inputs may be any that keep to these rules, and one draw needn't show every extreme that they name: `tile_columns`: slot s holds a tile column in [(s // 3) * 4, (s // 3 + 1) * 4); the slots of one row tile name distinct columns; a live slot's column is at most its row tile; the row tile's own column is always live, in the first slot of its group. `live_counts`: counts never exceed the columns allowed in that group, so the upper right region of groups is empty. In group 0 every row tile i >= 2 has exactly 3 live slots.
All inputs are finite; a program needn't handle non-finite values.
Results may differ from the reference program's by a relative error of at most 0.002.
Values may be sent and summed in bfloat16 or wider, within the bound.
No kernel may reach another device: no remote copies, remote signals or barrier semaphores. Data moves between devices by JAX's collectives and lax.ppermute only.
A program may use at most 64 MiB of HBM per device.

```python
import jax
import jax.numpy as jnp
from jax import lax

TILE = 256
CT = 4
K_C = 3
NV = 512
NB = 128
SLOTS = 96
ORDER = 32768
N_COL = 32


def draw_tile_columns(key, part):
    row_ids = jnp.arange(NB, dtype=jnp.int32)[:, None, None]
    group_ids = jnp.arange(N_COL, dtype=jnp.int32)[None, :, None]
    local_ids = jnp.arange(CT, dtype=jnp.int32)[None, None, :]
    reach = row_ids - group_ids * CT
    noise = jax.random.randint(key, (NB, N_COL, CT), 0, 4096, dtype=jnp.int32)
    scores = noise * CT + local_ids
    scores = jnp.where(local_ids > reach, scores + 4096 * CT * 2, scores)
    scores = jnp.where(local_ids == reach, -1, scores)
    order = jnp.argsort(scores, axis=2, stable=True)[:, :, :K_C]
    return (order + group_ids * CT).reshape(NB, SLOTS).astype(jnp.int32)


def draw_live_counts(key, part):
    row_ids = jnp.arange(NB, dtype=jnp.int32)[:, None]
    group_ids = jnp.arange(N_COL, dtype=jnp.int32)[None, :]
    allowed = jnp.clip(row_ids - group_ids * CT + 1, 0, CT)
    chosen = jax.random.randint(key, (NB, N_COL), 1, K_C + 1, dtype=jnp.int32)
    chosen = jnp.where(group_ids == 0, K_C, chosen)
    return jnp.minimum(chosen, allowed).astype(jnp.int32)


def block_scale(rng, extent, cuts, low, high):
    loudness, own = 1.0, jax.random.fold_in(rng, 6)
    for axis_at, shards_of in cuts:
        heights = jnp.exp(jax.random.uniform(jax.random.fold_in(own, axis_at), (shards_of,), jnp.float32, low / len(cuts), high / len(cuts)))
        loudness = loudness * jnp.repeat(heights, extent[axis_at] // shards_of).reshape([-1 if axis == axis_at else 1 for axis in range(len(extent))])
    return loudness


def scatter_about(rng, extent, spread, most, split=(), held_as=jnp.bfloat16):
    values = spread * jax.random.normal(rng, extent, jnp.float32)
    if split:
        values = values * block_scale(rng, extent, split, -0.22, 0.18)
    return jnp.clip(values, -most, most).astype(held_as)


def setup_inputs(seed: int = 0) -> dict:
    arg_keys = jax.random.split(jax.random.key(seed), 5)
    vectors = scatter_about(arg_keys[0], (NV, ORDER), 1.0, 6.0, ((0, 16), (1, 32)))
    factor_tiles = scatter_about(arg_keys[1], (NB, SLOTS, TILE, TILE), (TILE * K_C * N_COL // 2) ** -0.5, 0.0546875, ((0, 16), (1, 32)))
    tile_columns = draw_tile_columns(jax.random.fold_in(arg_keys[4], 71), 0)
    live_counts = draw_live_counts(jax.random.fold_in(arg_keys[4], 71), 0)
    return {"vectors": vectors, "factor_tiles": factor_tiles, "tile_columns": tile_columns, "live_counts": live_counts}


def reference(vectors, factor_tiles, tile_columns, live_counts):
    slot_ids = jnp.arange(SLOTS, dtype=jnp.int32)
    live_mask = ((slot_ids % K_C)[None, :] < jnp.repeat(live_counts, K_C, axis=1)).astype(jnp.float32)
    blocks = vectors.reshape(NV, NB, TILE)

    def forward_row(index):
        picked = jnp.take(blocks, tile_columns[index], axis=1).astype(jnp.float32)
        picked = picked * live_mask[index][None, :, None]
        return jnp.einsum("sab,vsb->va", factor_tiles[index].astype(jnp.float32), picked,
                          precision=lax.Precision.HIGHEST)

    row_list = jnp.arange(NB, dtype=jnp.int32)
    rows_out = lax.map(forward_row, row_list)
    rowvals = jnp.transpose(rows_out, (1, 0, 2)).astype(jnp.bfloat16)

    def backward_row(total, index):
        weights = rowvals[:, index].astype(jnp.float32)
        contrib = jnp.einsum("sab,va->svb", factor_tiles[index].astype(jnp.float32), weights,
                             precision=lax.Precision.HIGHEST)
        contrib = contrib * live_mask[index][:, None, None]
        total = total.at[:, tile_columns[index]].add(jnp.transpose(contrib, (1, 0, 2)))
        return total, None

    start_total = jnp.zeros((NV, NB, TILE), jnp.float32)
    total, unused = lax.scan(backward_row, start_total, row_list)
    return total.reshape(NV, NB * TILE)
```

```python
import functools

import jax
import jax.numpy as jnp
from jax import lax
from jax.experimental import pallas as pl
from jax.experimental.pallas import tpu as pltpu
from jax.sharding import PartitionSpec as P

BF16, F32 = jnp.bfloat16, jnp.float32
VMEM_BYTES = 40 * 1024 * 1024
LANES = 128
UNIT_BITS = 14


def swapped(shard, groups, axes):
    return lax.all_to_all(
        shard, axes, split_axis=0, concat_axis=0, axis_index_groups=groups, tiled=True
    )


def forward_kernel(own_tab, other_tab, vec_ref, own_ref, other_ref, out_ref, picked, total):
    step = pl.program_id(0)
    steps = total.shape[0]
    count, tile = picked.shape[1], picked.shape[2]
    per_core = picked.shape[0] // 2

    @pl.when(step == 0)
    def _():
        for col in range(2 * per_core):
            lo = (col % per_core) * tile
            block = vec_ref[:, col // per_core, :, lo : lo + tile]
            picked[col] = block.reshape(count, tile)

    acc = None
    for tab, ref in ((own_tab, own_ref), (other_tab, other_ref)):
        for slot in range(ref.shape[1]):
            col = tab[step, slot]
            values = picked[jnp.maximum(col, 0)]
            values = jnp.where(col >= 0, values, jnp.zeros_like(values))
            term = lax.dot_general(
                values, ref[0, slot], (((1,), (1,)), ((), ())), preferred_element_type=F32
            )
            acc = term if acc is None else acc + term
    total[step] = acc

    @pl.when(step == steps - 1)
    def _():
        most = jnp.zeros((count, tile), F32)
        for t in range(steps):
            most = jnp.maximum(most, jnp.abs(total[t]))
        most = jnp.max(most, axis=1, keepdims=True)
        power = jnp.floor(jnp.log2(jnp.maximum(most, 1e-30))) + 1.0
        unit = jnp.exp2(UNIT_BITS - power)
        parts, rows = out_ref.shape[0], out_ref.shape[1]
        for t in range(steps):
            code = jnp.floor(total[t] * unit + 0.5).astype(jnp.int32).astype(jnp.int16)
            out_ref[:, :, t * tile : (t + 1) * tile] = code.reshape(parts, rows, tile)
        power = jnp.broadcast_to(power, (count, LANES)).astype(jnp.int32).astype(jnp.int16)
        out_ref[:, :, steps * tile :] = power.reshape(parts, rows, LANES)


def forward(own_tab, other_tab, vecs, own, other):
    steps, slots, tile, _ = own.shape
    rows, _, part, width = vecs.shape
    count = rows * part
    smem = pl.BlockSpec(memory_space=pltpu.SMEM)
    tiles = pl.BlockSpec((1, slots, tile, tile), lambda t: (t, 0, 0, 0))
    shape = (rows, part, steps * tile + LANES)
    return pl.pallas_call(
        forward_kernel,
        grid=(steps,),
        in_specs=[smem, smem, pl.BlockSpec(vecs.shape, lambda t: (0, 0, 0, 0)), tiles, tiles],
        out_specs=pl.BlockSpec(shape, lambda t: (0, 0, 0)),
        out_shape=jax.ShapeDtypeStruct(shape, jnp.int16),
        scratch_shapes=[
            pltpu.VMEM((2 * width // tile, count, tile), BF16),
            pltpu.VMEM((steps, count, tile), F32),
        ],
        compiler_params=pltpu.CompilerParams(vmem_limit_bytes=VMEM_BYTES),
        cost_estimate=pl.CostEstimate(
            flops=4 * steps * slots * tile * tile * count,
            bytes_accessed=4 * own.size,
            transcendentals=0,
        ),
    )(own_tab, other_tab, vecs, own, other)


def settle_kernel(code_ref, out_ref):
    copies, _, width = out_ref.shape
    total = None
    for k in range(code_ref.shape[0]):
        power = code_ref[k, :, width:].astype(jnp.int32).astype(F32)
        unit = jnp.exp2(power[:, :1] - UNIT_BITS)
        term = code_ref[k, :, :width].astype(jnp.int32).astype(F32) * unit
        total = term if total is None else total + term
    value = total.astype(BF16)
    for k in range(copies):
        out_ref[k] = value


def settle(codes):
    copies, part, width = codes.shape
    return pl.pallas_call(
        settle_kernel,
        out_shape=jax.ShapeDtypeStruct((copies, part, width - LANES), BF16),
        compiler_params=pltpu.CompilerParams(vmem_limit_bytes=VMEM_BYTES),
    )(codes)


def backward_kernel(own_tab, other_tab, row_ref, own_ref, other_ref, out_ref, total):
    step = pl.program_id(0)
    cols, count, tile = total.shape
    per_core = cols // 2

    @pl.when(step == 0)
    def _():
        total[...] = jnp.zeros_like(total)

    values = row_ref[...].reshape(count, tile)
    for tab, ref in ((own_tab, own_ref), (other_tab, other_ref)):
        for slot in range(ref.shape[1]):
            col = tab[step, slot]
            term = jnp.dot(values, ref[0, slot], preferred_element_type=F32)
            place = jnp.maximum(col, 0)
            total[place] += jnp.where(col >= 0, term, jnp.zeros_like(term))

    @pl.when(step == pl.num_programs(0) - 1)
    def _():
        rows, _, part, _ = out_ref.shape
        for col in range(cols):
            lo = (col % per_core) * tile
            block = total[col].astype(BF16).reshape(rows, part, tile)
            out_ref[:, col // per_core, :, lo : lo + tile] = block


def backward(own_tab, other_tab, rowvals, own, other, shape):
    steps, slots, tile, _ = own.shape
    rows, part, _ = rowvals.shape
    count = rows * part
    smem = pl.BlockSpec(memory_space=pltpu.SMEM)
    tiles = pl.BlockSpec((1, slots, tile, tile), lambda t: (t, 0, 0, 0))
    return pl.pallas_call(
        backward_kernel,
        grid=(steps,),
        in_specs=[smem, smem, pl.BlockSpec((rows, part, tile), lambda t: (0, 0, t)), tiles, tiles],
        out_specs=pl.BlockSpec(shape, lambda t: (0, 0, 0, 0)),
        out_shape=jax.ShapeDtypeStruct(shape, BF16),
        scratch_shapes=[pltpu.VMEM((2 * shape[3] // tile, count, tile), F32)],
        compiler_params=pltpu.CompilerParams(vmem_limit_bytes=VMEM_BYTES),
        cost_estimate=pl.CostEstimate(
            flops=4 * steps * slots * tile * tile * count,
            bytes_accessed=4 * own.size,
            transcendentals=0,
        ),
    )(own_tab, other_tab, rowvals, own, other)


def per_device(n_row, n_col, vectors, factor_tiles, tile_columns, live_counts):
    _, slots, tile, _ = factor_tiles.shape
    chips = n_col // 2
    part = vectors.shape[0] // 2
    width = vectors.shape[1]
    col_tiles = width // tile
    pairs = [(c, c ^ 1) for c in range(n_col)]
    same_core = [[core + 2 * p for p in range(chips)] for core in range(2)]
    row_core = [
        [r * n_col + 2 * p + core for r in range(n_row) for core in range(2)] for p in range(chips)
    ]

    chip = lax.axis_index("col") // 2
    slot_index = lax.broadcasted_iota(jnp.int32, tile_columns.shape, 1)
    local = tile_columns - chip * (2 * col_tiles)
    own_tab = jnp.where(slot_index < live_counts, local, -1)
    other_tab = lax.ppermute(own_tab, "col", pairs)
    other_tiles = lax.ppermute(factor_tiles, "col", pairs)

    copies = jnp.broadcast_to(vectors, (n_row, 2 * part, width)).reshape(2 * n_row, part, width)
    gathered = swapped(copies, row_core, ("row", "col")).reshape(n_row, 2, part, width)

    codes = forward(own_tab, other_tab, gathered, factor_tiles, other_tiles)
    rowvals = settle(swapped(codes, same_core, "col"))
    rowvals = swapped(rowvals, same_core, "col")

    sums = backward(own_tab, other_tab, rowvals, factor_tiles, other_tiles, gathered.shape)
    sums = swapped(sums.reshape(2 * n_row, part, width), row_core, ("row", "col"))
    return sums.reshape(n_row, 2 * part, width).astype(F32).sum(axis=0)


def solution(mesh):
    in_specs = (P("row", "col"), P("row", "col", None, None), P("row", "col"), P("row", "col"))
    body = functools.partial(per_device, mesh.shape["row"], mesh.shape["col"])
    return jax.shard_map(
        body, mesh=mesh, in_specs=in_specs, out_specs=P("row", "col"), check_vma=False
    )
```

```python
import functools

import jax
import jax.numpy as jnp
from jax import lax
from jax.experimental import pallas as pl
from jax.experimental.pallas import tpu as pltpu
from jax.sharding import PartitionSpec as P

BF16, F32 = jnp.bfloat16, jnp.float32
VMEM_BYTES = 24 * 1024 * 1024
LANES = 128
UNIT_BITS = 14
PIECES = 2


def swapped(shard, groups, axes):
    return lax.all_to_all(
        shard, axes, split_axis=0, concat_axis=0, axis_index_groups=groups, tiled=True
    )


SMEM = pl.BlockSpec(memory_space=pltpu.SMEM)
VMEM = pl.BlockSpec(memory_space=pltpu.VMEM)
ANY = pl.BlockSpec(memory_space=pl.ANY)


def params():
    return pltpu.CompilerParams(vmem_limit_bytes=VMEM_BYTES)


def cost(factor, count):
    slots = 2 * factor.shape[0] * factor.shape[1]
    tile = factor.shape[2]
    return pl.CostEstimate(
        flops=2 * slots * tile * tile * count,
        bytes_accessed=2 * slots * tile * tile,
        transcendentals=0,
    )


def spread_kernel(vec_ref, out_ref):
    for copy in range(out_ref.shape[0]):
        out_ref[copy] = vec_ref[...]


def spread(vectors, copies):
    return pl.pallas_call(
        spread_kernel,
        in_specs=[VMEM],
        out_specs=VMEM,
        out_shape=jax.ShapeDtypeStruct((copies, *vectors.shape), vectors.dtype),
        compiler_params=params(),
    )(vectors)


def fetches(sources, held, sems):
    depth = sources[0].shape[0]
    return [
        pltpu.make_async_copy(ref, held.at[k * depth : (k + 1) * depth], sems.at[k])
        for k, ref in enumerate(sources)
    ]


def forward_kernel(core_ref, own_tab, other_tab, vec_ref, own_ref, *refs):
    sources, (out_ref, picked, total, other_ref, sems) = refs[:PIECES], refs[PIECES:]
    steps, count, tile = total.shape
    per_core = picked.shape[0] // 2
    core = core_ref[0]
    copies = fetches(sources, other_ref, sems)
    for copy in copies:
        copy.start()
    for col in range(2 * per_core):
        lo = (col % per_core) * tile
        picked[col] = vec_ref[:, col // per_core, :, lo : lo + tile].reshape(count, tile)

    most = jnp.zeros((count, tile), F32)
    for tab, ref, side in ((own_tab, own_ref, core), (other_tab, other_ref, 1 - core)):
        if ref is other_ref:
            for copy in copies:
                copy.wait()
        for step in range(steps):
            acc = total[step] if ref is other_ref else None
            for slot in range(ref.shape[1]):
                col = tab[step, slot]
                values = picked[side * per_core + jnp.maximum(col, 0)]
                values = jnp.where(col >= 0, values, jnp.zeros_like(values))
                term = lax.dot_general(
                    values, ref[step, slot], (((1,), (1,)), ((), ())), preferred_element_type=F32
                )
                acc = term if acc is None else acc + term
            total[step] = acc
            if ref is other_ref:
                most = jnp.maximum(most, jnp.abs(acc))

    most = jnp.max(most, axis=1, keepdims=True)
    power = jnp.floor(jnp.log2(jnp.maximum(most, 1e-30))) + 1.0
    unit = jnp.exp2(UNIT_BITS - power)
    parts, rows = out_ref.shape[0], out_ref.shape[1]
    for step in range(steps):
        code = jnp.floor(total[step] * unit + 0.5).astype(jnp.int32).astype(jnp.int16)
        out_ref[:, :, step * tile : (step + 1) * tile] = code.reshape(parts, rows, tile)
    power = jnp.broadcast_to(power, (count, LANES)).astype(jnp.int32).astype(jnp.int16)
    out_ref[:, :, steps * tile :] = power.reshape(parts, rows, LANES)


def forward(core, own_tab, other_tab, vecs, own, other):
    steps, _, tile, _ = own.shape
    rows, _, part, width = vecs.shape
    count = rows * part
    return pl.pallas_call(
        forward_kernel,
        in_specs=[SMEM] * 3 + [VMEM] * 2 + [ANY] * PIECES,
        out_specs=VMEM,
        out_shape=jax.ShapeDtypeStruct((rows, part, steps * tile + LANES), jnp.int16),
        scratch_shapes=[
            pltpu.VMEM((2 * width // tile, count, tile), BF16),
            pltpu.VMEM((steps, count, tile), F32),
            pltpu.VMEM(own.shape, BF16),
            pltpu.SemaphoreType.DMA((PIECES,)),
        ],
        compiler_params=params(),
        cost_estimate=cost(own, count),
    )(core, own_tab, other_tab, vecs, own, *other)


def settle_kernel(code_ref, out_ref):
    copies, _, width = out_ref.shape
    total = None
    for k in range(code_ref.shape[0]):
        power = code_ref[k, :, width:].astype(jnp.int32).astype(F32)
        unit = jnp.exp2(power[:, :1] - UNIT_BITS)
        term = code_ref[k, :, :width].astype(jnp.int32).astype(F32) * unit
        total = term if total is None else total + term
    value = total.astype(BF16)
    for k in range(copies):
        out_ref[k] = value


def settle(codes):
    copies, part, width = codes.shape
    return pl.pallas_call(
        settle_kernel,
        in_specs=[VMEM],
        out_specs=VMEM,
        out_shape=jax.ShapeDtypeStruct((copies, part, width - LANES), BF16),
        compiler_params=params(),
    )(codes)


def backward_kernel(core_ref, own_tab, other_tab, row_ref, own_ref, *refs):
    sources, (out_ref, other_ref, sems) = refs[:PIECES], refs[PIECES:]
    rows, _, part, width = out_ref.shape
    steps, slots, tile, _ = own_ref.shape
    core = core_ref[0]
    copies = fetches(sources, other_ref, sems)
    for copy in copies:
        copy.start()
    for tab, ref, side in ((own_tab, own_ref, core), (other_tab, other_ref, 1 - core)):
        if ref is other_ref:
            for copy in copies:
                copy.wait()
        for col in range(width // tile):
            acc = None
            for step in range(steps):
                slot = jnp.int32(-1)
                for s in range(slots):
                    slot = jnp.where(tab[step, s] == col, s, slot)
                values = row_ref[:, :, step * tile : (step + 1) * tile].reshape(rows * part, tile)
                values = jnp.where(slot >= 0, values, jnp.zeros_like(values))
                term = jnp.dot(
                    values, ref[step, jnp.maximum(slot, 0)], preferred_element_type=F32
                )
                acc = term if acc is None else acc + term
            block = acc.astype(BF16).reshape(rows, part, tile)
            out_ref[:, side, :, col * tile : (col + 1) * tile] = block


def backward(core, own_tab, other_tab, rowvals, own, other, shape):
    return pl.pallas_call(
        backward_kernel,
        in_specs=[SMEM] * 3 + [VMEM] * 2 + [ANY] * PIECES,
        out_specs=VMEM,
        out_shape=jax.ShapeDtypeStruct(shape, BF16),
        scratch_shapes=[pltpu.VMEM(own.shape, BF16), pltpu.SemaphoreType.DMA((PIECES,))],
        compiler_params=params(),
        cost_estimate=cost(own, rowvals.shape[0] * rowvals.shape[1]),
    )(core, own_tab, other_tab, rowvals, own, *other)


def per_device(n_row, n_col, vectors, factor_tiles, tile_columns, live_counts):
    part = vectors.shape[0] // 2
    width = vectors.shape[1]
    col_tiles = width // factor_tiles.shape[2]
    chips = n_col // 2
    pairs = [(c, c ^ 1) for c in range(n_col)]
    same_core = [[core + 2 * p for p in range(chips)] for core in range(2)]
    row_core = [
        [r * n_col + 2 * p + core for r in range(n_row) for core in range(2)] for p in range(chips)
    ]

    col = lax.axis_index("col")
    core = (col & 1).reshape(1)
    copies = spread(vectors, n_row).reshape(2 * n_row, part, width)
    gathered = swapped(copies, row_core, ("row", "col")).reshape(n_row, 2, part, width)

    slot_index = lax.broadcasted_iota(jnp.int32, tile_columns.shape, 1)
    own_tab = jnp.where(slot_index < live_counts, tile_columns - col * col_tiles, -1)
    other_tab = lax.ppermute(own_tab, "col", pairs)
    other_tiles = []
    for piece in jnp.split(factor_tiles, PIECES):
        piece, other_tab = lax.optimization_barrier((piece, other_tab))
        other_tiles.append(lax.ppermute(piece, "col", pairs))

    codes = forward(core, own_tab, other_tab, gathered, factor_tiles, other_tiles)
    rowvals = settle(swapped(codes, same_core, "col"))
    rowvals = swapped(rowvals, same_core, "col")

    sums = backward(core, own_tab, other_tab, rowvals, factor_tiles, other_tiles, gathered.shape)
    sums = swapped(sums.reshape(2 * n_row, part, width), row_core, ("row", "col"))
    return sums.reshape(n_row, 2 * part, width).astype(F32).sum(axis=0)


def solution(mesh):
    in_specs = (P("row", "col"), P("row", "col", None, None), P("row", "col"), P("row", "col"))
    body = functools.partial(per_device, mesh.shape["row"], mesh.shape["col"])
    return jax.shard_map(
        body, mesh=mesh, in_specs=in_specs, out_specs=P("row", "col"), check_vma=False
    )
```

```python
import functools

import jax
import jax.numpy as jnp
from jax import lax
from jax.experimental import pallas as pl
from jax.experimental.pallas import tpu as pltpu
from jax.sharding import PartitionSpec as P

BF16, F32 = jnp.bfloat16, jnp.float32
VMEM_BYTES = 24 * 1024 * 1024
WIDE_BYTES = 48 * 1024 * 1024
LANES = 128
WIDEST_BYTES = 58 * 1024 * 1024
UNIT_BITS = 14
PIECES = 2


def swapped(shard, groups, axes):
    return lax.all_to_all(
        shard, axes, split_axis=0, concat_axis=0, axis_index_groups=groups, tiled=True
    )


SMEM = pl.BlockSpec(memory_space=pltpu.SMEM)
VMEM = pl.BlockSpec(memory_space=pltpu.VMEM)
ANY = pl.BlockSpec(memory_space=pl.ANY)


def params(limit=VMEM_BYTES):
    return pltpu.CompilerParams(vmem_limit_bytes=limit)


def cost(factor, count):
    return pl.CostEstimate(
        flops=2 * factor.size * count, bytes_accessed=2 * factor.size, transcendentals=0
    )


def spread_kernel(vec_ref, out_ref, sems):
    copies = [
        pltpu.make_async_copy(vec_ref, out_ref.at[k], sems.at[k]) for k in range(out_ref.shape[0])
    ]
    for copy in copies:
        copy.start()
    for copy in copies:
        copy.wait()


def spread(vectors, copies):
    return pl.pallas_call(
        spread_kernel,
        in_specs=[ANY],
        out_specs=ANY,
        out_shape=jax.ShapeDtypeStruct((copies, *vectors.shape), vectors.dtype),
        scratch_shapes=[pltpu.SemaphoreType.DMA((copies,))],
        compiler_params=params(WIDEST_BYTES),
    )(vectors)


def dense_kernel(own_tab, other_tab, own_ref, *refs):
    other_refs, out_ref = refs[:PIECES], refs[PIECES]
    step = pl.program_id(0)
    piece = step // (pl.num_programs(0) // PIECES)
    slots = own_ref.shape[1]
    cols = out_ref.shape[0] // 2
    for side, (tab, sources) in enumerate(((own_tab, [own_ref]), (other_tab, other_refs))):
        for col in range(cols):
            slot = jnp.int32(-1)
            for s in range(slots):
                slot = jnp.where(tab[step, s] == col, s, slot)
            block = jnp.zeros(out_ref.shape[1:], BF16)
            for k, ref in enumerate(sources):
                chosen = slot >= 0 if len(sources) == 1 else (slot >= 0) & (piece == k)
                block = jnp.where(chosen, ref[0, jnp.maximum(slot, 0)], block)
            out_ref[side * cols + col] = block


def dense(own_tab, other_tab, own, other, cols):
    steps, slots, tile, _ = own.shape
    depth = steps // PIECES
    tiles = [pl.BlockSpec((1, slots, tile, tile), lambda t: (t, 0, 0, 0))]
    for k in range(PIECES):
        place = lambda t, k=k: (jnp.clip(t - k * depth, 0, depth - 1), 0, 0, 0)
        tiles.append(pl.BlockSpec((1, slots, tile, tile), place))
    return pl.pallas_call(
        dense_kernel,
        grid=(steps,),
        in_specs=[SMEM, SMEM, *tiles],
        out_specs=pl.BlockSpec((2 * cols, tile, tile), lambda t: (0, t, 0)),
        out_shape=jax.ShapeDtypeStruct((2 * cols, steps * tile, tile), BF16),
        compiler_params=params(WIDE_BYTES),
        cost_estimate=pl.CostEstimate(flops=0, bytes_accessed=8 * own.size, transcendentals=0),
    )(own_tab, other_tab, own, *other)


def forward_kernel(core_ref, vec_ref, source_ref, out_ref, held, total, factor_ref, sems):
    rows, _, part, width = vec_ref.shape
    count = rows * part
    steps = total.shape[0]
    tile = total.shape[2]
    core = core_ref[0]
    strips = [pl.ds(step * tile, tile) for step in range(steps)]
    copies = [
        pltpu.make_async_copy(source_ref.at[:, strip], factor_ref.at[:, strip], sems.at[step])
        for step, strip in enumerate(strips)
    ]
    for copy in copies:
        copy.start()
    held[:, :width] = vec_ref[:, core].reshape(count, width)
    held[:, width:] = vec_ref[:, 1 - core].reshape(count, width)
    most = jnp.zeros((count, tile), F32)
    for step in range(steps):
        copies[step].wait()
        acc = None
        for col in range(factor_ref.shape[0]):
            term = lax.dot_general(
                held[:, col * tile : (col + 1) * tile],
                factor_ref[col, strips[step], :],
                (((1,), (1,)), ((), ())),
                preferred_element_type=F32,
            )
            acc = term if acc is None else acc + term
        total[step] = acc
        most = jnp.maximum(most, jnp.abs(acc))

    most = jnp.max(most, axis=1, keepdims=True)
    power = jnp.floor(jnp.log2(jnp.maximum(most, 1e-30))) + 1.0
    unit = jnp.exp2(UNIT_BITS - power)
    for step in range(steps):
        code = jnp.floor(total[step] * unit + 0.5).astype(jnp.int32).astype(jnp.int16)
        out_ref[:, :, step * tile : (step + 1) * tile] = code.reshape(rows, part, tile)
    power = jnp.broadcast_to(power, (count, LANES)).astype(jnp.int32).astype(jnp.int16)
    out_ref[:, :, steps * tile :] = power.reshape(rows, part, LANES)


def forward(core, vecs, factor):
    rows, _, part, width = vecs.shape
    count = rows * part
    _, height, tile = factor.shape
    return pl.pallas_call(
        forward_kernel,
        in_specs=[SMEM, VMEM, ANY],
        out_specs=VMEM,
        out_shape=jax.ShapeDtypeStruct((rows, part, height + LANES), jnp.int16),
        scratch_shapes=[
            pltpu.VMEM((count, 2 * width), BF16),
            pltpu.VMEM((height // tile, count, tile), F32),
            pltpu.VMEM(factor.shape, BF16),
            pltpu.SemaphoreType.DMA((height // tile,)),
        ],
        compiler_params=params(WIDE_BYTES),
        cost_estimate=cost(factor, count),
    )(core, vecs, factor)


def settle_kernel(code_ref, out_ref):
    copies, _, width = out_ref.shape
    total = None
    for k in range(code_ref.shape[0]):
        power = code_ref[k, :, width:].astype(jnp.int32).astype(F32)
        unit = jnp.exp2(power[:, :1] - UNIT_BITS)
        term = code_ref[k, :, :width].astype(jnp.int32).astype(F32) * unit
        total = term if total is None else total + term
    value = total.astype(BF16)
    for k in range(copies):
        out_ref[k] = value


def settle(codes):
    copies, part, width = codes.shape
    return pl.pallas_call(
        settle_kernel,
        in_specs=[VMEM],
        out_specs=VMEM,
        out_shape=jax.ShapeDtypeStruct((copies, part, width - LANES), BF16),
        compiler_params=params(),
    )(codes)


def backward_kernel(core_ref, row_ref, source_ref, out_ref, factor_ref, sems):
    rows, _, part, _ = out_ref.shape
    cols, _, tile = factor_ref.shape
    core = core_ref[0]
    copies = [
        pltpu.make_async_copy(source_ref.at[col], factor_ref.at[col], sems.at[col])
        for col in range(cols)
    ]
    for copy in copies:
        copy.start()
    values = row_ref[...].reshape(rows * part, row_ref.shape[2])
    for col in range(cols):
        copies[col].wait()
        place = core if col < cols // 2 else 1 - core
        lo = col % (cols // 2) * tile
        block = jnp.dot(values, factor_ref[col], preferred_element_type=F32)
        out_ref[:, place, :, lo : lo + tile] = block.astype(BF16).reshape(rows, part, tile)


def backward(core, rowvals, factor, shape):
    return pl.pallas_call(
        backward_kernel,
        in_specs=[SMEM, VMEM, ANY],
        out_specs=VMEM,
        out_shape=jax.ShapeDtypeStruct(shape, BF16),
        scratch_shapes=[
            pltpu.VMEM(factor.shape, BF16),
            pltpu.SemaphoreType.DMA((factor.shape[0],)),
        ],
        compiler_params=params(WIDE_BYTES),
        cost_estimate=cost(factor, rowvals.shape[0] * rowvals.shape[1]),
    )(core, rowvals, factor)


def per_device(n_row, n_col, vectors, factor_tiles, tile_columns, live_counts):
    part = vectors.shape[0] // 2
    width = vectors.shape[1]
    col_tiles = width // factor_tiles.shape[2]
    chips = n_col // 2
    pairs = [(c, c ^ 1) for c in range(n_col)]
    same_core = [[core + 2 * p for p in range(chips)] for core in range(2)]
    row_core = [
        [r * n_col + 2 * p + core for r in range(n_row) for core in range(2)] for p in range(chips)
    ]

    col = lax.axis_index("col")
    core = (col & 1).reshape(1)
    copies = spread(vectors, n_row).reshape(2 * n_row, part, width)
    gathered = swapped(copies, row_core, ("row", "col")).reshape(n_row, 2, part, width)

    slot_index = lax.broadcasted_iota(jnp.int32, tile_columns.shape, 1)
    own_tab = jnp.where(slot_index < live_counts, tile_columns - col * col_tiles, -1)
    other_tab = lax.ppermute(own_tab, "col", pairs)
    other_tiles = []
    for piece in jnp.split(factor_tiles, PIECES):
        piece, other_tab = lax.optimization_barrier((piece, other_tab))
        other_tiles.append(lax.ppermute(piece, "col", pairs))

    factor = dense(own_tab, other_tab, factor_tiles, other_tiles, col_tiles)
    codes = forward(core, gathered, factor)
    rowvals = settle(swapped(codes, same_core, "col"))
    rowvals = swapped(rowvals, same_core, "col")

    sums = backward(core, rowvals, factor, gathered.shape)
    sums = swapped(sums.reshape(2 * n_row, part, width), row_core, ("row", "col"))
    return sums.reshape(n_row, 2 * part, width).astype(F32).sum(axis=0)


def solution(mesh):
    in_specs = (P("row", "col"), P("row", "col", None, None), P("row", "col"), P("row", "col"))
    body = functools.partial(per_device, mesh.shape["row"], mesh.shape["col"])
    return jax.shard_map(
        body, mesh=mesh, in_specs=in_specs, out_specs=P("row", "col"), check_vma=False
    )
```

```python
import functools

import jax
import jax.numpy as jnp
from jax import lax
from jax.experimental import pallas as pl
from jax.experimental.pallas import tpu as pltpu
from jax.sharding import PartitionSpec as P

BF16, F32 = jnp.bfloat16, jnp.float32
VMEM_BYTES = 24 * 1024 * 1024
LANES = 128
UNIT_BITS = 14
PIECES = 2


def swapped(shard, groups, axes):
    return lax.all_to_all(
        shard, axes, split_axis=0, concat_axis=0, axis_index_groups=groups, tiled=True
    )


SMEM = pl.BlockSpec(memory_space=pltpu.SMEM)
VMEM = pl.BlockSpec(memory_space=pltpu.VMEM)
ANY = pl.BlockSpec(memory_space=pl.ANY)


def params():
    return pltpu.CompilerParams(vmem_limit_bytes=VMEM_BYTES)


def cost(factor, count):
    return pl.CostEstimate(
        flops=2 * factor.size * count, bytes_accessed=2 * factor.size, transcendentals=0
    )


def spread_kernel(vec_ref, out_ref):
    for copy in range(out_ref.shape[0]):
        out_ref[copy] = vec_ref[...]


def spread(vectors, copies):
    return pl.pallas_call(
        spread_kernel,
        in_specs=[VMEM],
        out_specs=VMEM,
        out_shape=jax.ShapeDtypeStruct((copies, *vectors.shape), vectors.dtype),
        compiler_params=params(),
    )(vectors)


def fetches(sources, held, sems):
    depth = sources[0].shape[0]
    return [
        pltpu.make_async_copy(ref, held.at[k * depth : (k + 1) * depth], sems.at[k])
        for k, ref in enumerate(sources)
    ]


def forward_kernel(core_ref, own_tab, other_tab, vec_ref, own_ref, *refs):
    sources, (out_ref, picked, total, other_ref, sems) = refs[:PIECES], refs[PIECES:]
    steps, count, tile = total.shape
    per_core = picked.shape[0] // 2
    core = core_ref[0]
    copies = fetches(sources, other_ref, sems)
    for copy in copies:
        copy.start()
    for col in range(2 * per_core):
        lo = (col % per_core) * tile
        picked[col] = vec_ref[:, col // per_core, :, lo : lo + tile].reshape(count, tile)

    most = jnp.zeros((count, tile), F32)
    for tab, ref, side in ((own_tab, own_ref, core), (other_tab, other_ref, 1 - core)):
        if ref is other_ref:
            for copy in copies:
                copy.wait()
        for step in range(steps):
            acc = total[step] if ref is other_ref else None
            for slot in range(ref.shape[1]):
                col = tab[step, slot]
                values = picked[side * per_core + jnp.maximum(col, 0)]
                values = jnp.where(col >= 0, values, jnp.zeros_like(values))
                term = lax.dot_general(
                    values, ref[step, slot], (((1,), (1,)), ((), ())), preferred_element_type=F32
                )
                acc = term if acc is None else acc + term
            total[step] = acc
            if ref is other_ref:
                most = jnp.maximum(most, jnp.abs(acc))

    most = jnp.max(most, axis=1, keepdims=True)
    power = jnp.floor(jnp.log2(jnp.maximum(most, 1e-30))) + 1.0
    unit = jnp.exp2(UNIT_BITS - power)
    parts, rows = out_ref.shape[0], out_ref.shape[1]
    for step in range(steps):
        code = jnp.floor(total[step] * unit + 0.5).astype(jnp.int32).astype(jnp.int16)
        out_ref[:, :, step * tile : (step + 1) * tile] = code.reshape(parts, rows, tile)
    power = jnp.broadcast_to(power, (count, LANES)).astype(jnp.int32).astype(jnp.int16)
    out_ref[:, :, steps * tile :] = power.reshape(parts, rows, LANES)


def forward(core, own_tab, other_tab, vecs, own, other):
    steps, _, tile, _ = own.shape
    rows, _, part, width = vecs.shape
    count = rows * part
    return pl.pallas_call(
        forward_kernel,
        in_specs=[SMEM] * 3 + [VMEM] * 2 + [ANY] * PIECES,
        out_specs=VMEM,
        out_shape=jax.ShapeDtypeStruct((rows, part, steps * tile + LANES), jnp.int16),
        scratch_shapes=[
            pltpu.VMEM((2 * width // tile, count, tile), BF16),
            pltpu.VMEM((steps, count, tile), F32),
            pltpu.VMEM(own.shape, BF16),
            pltpu.SemaphoreType.DMA((PIECES,)),
        ],
        compiler_params=params(),
        cost_estimate=cost(own, 2 * count),
    )(core, own_tab, other_tab, vecs, own, *other)


def dense_kernel(own_tab, other_tab, own_ref, *refs):
    other_refs, out_ref = refs[:PIECES], refs[PIECES]
    step = pl.program_id(0)
    piece = step // (pl.num_programs(0) // PIECES)
    slots = own_ref.shape[1]
    cols = out_ref.shape[0] // 2
    for side, (tab, sources) in enumerate(((own_tab, [own_ref]), (other_tab, other_refs))):
        for col in range(cols):
            slot = jnp.int32(-1)
            for s in range(slots):
                slot = jnp.where(tab[step, s] == col, s, slot)
            block = jnp.zeros(out_ref.shape[1:], BF16)
            for k, ref in enumerate(sources):
                chosen = slot >= 0 if len(sources) == 1 else (slot >= 0) & (piece == k)
                block = jnp.where(chosen, ref[0, jnp.maximum(slot, 0)], block)
            out_ref[side * cols + col] = block


def dense(own_tab, other_tab, own, other, cols):
    steps, slots, tile, _ = own.shape
    depth = steps // PIECES
    tiles = [pl.BlockSpec((1, slots, tile, tile), lambda t: (t, 0, 0, 0))]
    for k in range(PIECES):
        place = lambda t, k=k: (jnp.clip(t - k * depth, 0, depth - 1), 0, 0, 0)
        tiles.append(pl.BlockSpec((1, slots, tile, tile), place))
    return pl.pallas_call(
        dense_kernel,
        grid=(steps,),
        in_specs=[SMEM, SMEM, *tiles],
        out_specs=pl.BlockSpec((2 * cols, tile, tile), lambda t: (0, t, 0)),
        out_shape=jax.ShapeDtypeStruct((2 * cols, steps * tile, tile), BF16),
        compiler_params=params(),
        cost_estimate=pl.CostEstimate(flops=0, bytes_accessed=8 * own.size, transcendentals=0),
    )(own_tab, other_tab, own, *other)


def settle_kernel(code_ref, out_ref):
    copies, _, width = out_ref.shape
    total = None
    for k in range(code_ref.shape[0]):
        power = code_ref[k, :, width:].astype(jnp.int32).astype(F32)
        unit = jnp.exp2(power[:, :1] - UNIT_BITS)
        term = code_ref[k, :, :width].astype(jnp.int32).astype(F32) * unit
        total = term if total is None else total + term
    value = total.astype(BF16)
    for k in range(copies):
        out_ref[k] = value


def settle(codes):
    copies, part, width = codes.shape
    return pl.pallas_call(
        settle_kernel,
        in_specs=[VMEM],
        out_specs=VMEM,
        out_shape=jax.ShapeDtypeStruct((copies, part, width - LANES), BF16),
        compiler_params=params(),
    )(codes)


def backward_kernel(core_ref, row_ref, factor_ref, out_ref):
    rows, _, part, _ = out_ref.shape
    cols, _, tile = factor_ref.shape
    core = core_ref[0]
    values = row_ref[...].reshape(rows * part, row_ref.shape[2])
    for col in range(cols):
        place = core if col < cols // 2 else 1 - core
        lo = col % (cols // 2) * tile
        block = jnp.dot(values, factor_ref[col], preferred_element_type=F32)
        out_ref[:, place, :, lo : lo + tile] = block.astype(BF16).reshape(rows, part, tile)


def backward(core, rowvals, factor, shape):
    return pl.pallas_call(
        backward_kernel,
        in_specs=[SMEM, VMEM, VMEM],
        out_specs=VMEM,
        out_shape=jax.ShapeDtypeStruct(shape, BF16),
        compiler_params=params(),
        cost_estimate=cost(factor, rowvals.shape[0] * rowvals.shape[1]),
    )(core, rowvals, factor)


def per_device(n_row, n_col, vectors, factor_tiles, tile_columns, live_counts):
    part = vectors.shape[0] // 2
    width = vectors.shape[1]
    col_tiles = width // factor_tiles.shape[2]
    chips = n_col // 2
    pairs = [(c, c ^ 1) for c in range(n_col)]
    same_core = [[core + 2 * p for p in range(chips)] for core in range(2)]
    row_core = [
        [r * n_col + 2 * p + core for r in range(n_row) for core in range(2)] for p in range(chips)
    ]

    col = lax.axis_index("col")
    core = (col & 1).reshape(1)
    copies = spread(vectors, n_row).reshape(2 * n_row, part, width)
    gathered = swapped(copies, row_core, ("row", "col")).reshape(n_row, 2, part, width)

    slot_index = lax.broadcasted_iota(jnp.int32, tile_columns.shape, 1)
    own_tab = jnp.where(slot_index < live_counts, tile_columns - col * col_tiles, -1)
    other_tab = lax.ppermute(own_tab, "col", pairs)
    other_tiles = []
    for piece in jnp.split(factor_tiles, PIECES):
        piece, other_tab = lax.optimization_barrier((piece, other_tab))
        other_tiles.append(lax.ppermute(piece, "col", pairs))

    factor = dense(own_tab, other_tab, factor_tiles, other_tiles, col_tiles)
    gathered, factor = lax.optimization_barrier((gathered, factor))
    codes = forward(core, own_tab, other_tab, gathered, factor_tiles, other_tiles)
    rowvals = settle(swapped(codes, same_core, "col"))
    rowvals = swapped(rowvals, same_core, "col")

    sums = backward(core, rowvals, factor, gathered.shape)
    sums = swapped(sums.reshape(2 * n_row, part, width), row_core, ("row", "col"))
    return sums.reshape(n_row, 2 * part, width).astype(F32).sum(axis=0)


def solution(mesh):
    in_specs = (P("row", "col"), P("row", "col", None, None), P("row", "col"), P("row", "col"))
    body = functools.partial(per_device, mesh.shape["row"], mesh.shape["col"])
    return jax.shard_map(
        body, mesh=mesh, in_specs=in_specs, out_specs=P("row", "col"), check_vma=False
    )
```

```python
import functools

import jax
import jax.numpy as jnp
from jax import lax
from jax.experimental import pallas as pl
from jax.experimental.pallas import tpu as pltpu
from jax.sharding import PartitionSpec as P

BF16, F32 = jnp.bfloat16, jnp.float32
VMEM_BYTES = 24 * 1024 * 1024
LANES = 128
UNIT_BITS = 14
PIECES = 2


def swapped(shard, groups, axes):
    return lax.all_to_all(
        shard, axes, split_axis=0, concat_axis=0, axis_index_groups=groups, tiled=True
    )


SMEM = pl.BlockSpec(memory_space=pltpu.SMEM)
VMEM = pl.BlockSpec(memory_space=pltpu.VMEM)
ANY = pl.BlockSpec(memory_space=pl.ANY)


def params():
    return pltpu.CompilerParams(vmem_limit_bytes=VMEM_BYTES)


def cost(factor, count):
    return pl.CostEstimate(
        flops=2 * factor.size * count, bytes_accessed=2 * factor.size, transcendentals=0
    )


def spread_kernel(vec_ref, out_ref):
    for copy in range(out_ref.shape[0]):
        out_ref[copy] = vec_ref[...]


def spread(vectors, copies):
    return pl.pallas_call(
        spread_kernel,
        in_specs=[VMEM],
        out_specs=VMEM,
        out_shape=jax.ShapeDtypeStruct((copies, *vectors.shape), vectors.dtype),
        compiler_params=params(),
    )(vectors)


def fetches(sources, held, sems):
    depth = sources[0].shape[0]
    return [
        pltpu.make_async_copy(ref, held.at[k * depth : (k + 1) * depth], sems.at[k])
        for k, ref in enumerate(sources)
    ]


def forward_kernel(core_ref, own_tab, other_tab, vec_source, own_ref, *refs):
    sources, (out_ref, vec_ref, picked, total, other_ref, sems) = refs[:PIECES], refs[PIECES:]
    steps, count, tile = total.shape
    per_core = (picked.shape[0] - 1) // 2
    core = core_ref[0]
    copies = [
        pltpu.make_async_copy(vec_source.at[:, side], vec_ref.at[k], sems.at[PIECES + k])
        for k, side in enumerate((core, 1 - core))
    ] + fetches(sources, other_ref, sems)
    for copy in copies:
        copy.start()
    picked[2 * per_core] = jnp.zeros((count, tile), BF16)

    most = jnp.zeros((count, tile), F32)
    for side, (tab, ref) in enumerate(((own_tab, own_ref), (other_tab, other_ref))):
        for copy in copies[1:] if side else copies[:1]:
            copy.wait()
        for col in range(per_core):
            block = vec_ref[side, :, :, col * tile : (col + 1) * tile]
            picked[side * per_core + col] = block.reshape(count, tile)
        for step in range(steps):
            acc = total[step] if side else None
            for slot in range(ref.shape[1]):
                col = tab[step, slot]
                values = picked[jnp.where(col >= 0, side * per_core + col, 2 * per_core)]
                term = lax.dot_general(
                    values, ref[step, slot], (((1,), (1,)), ((), ())), preferred_element_type=F32
                )
                acc = term if acc is None else acc + term
            total[step] = acc
            if side:
                most = jnp.maximum(most, jnp.abs(acc))

    most = jnp.max(most, axis=1, keepdims=True)
    power = jnp.floor(jnp.log2(jnp.maximum(most, 1e-30))) + 1.0
    unit = jnp.exp2(UNIT_BITS - power)
    parts = out_ref.shape[0]
    rows = count // parts
    for step in range(steps):
        code = jnp.floor(total[step] * unit + 0.5).astype(jnp.int32).astype(jnp.int16)
        for half in range(tile // LANES):
            at = (step * (tile // LANES) + half) * rows
            block = code[:, half * LANES : (half + 1) * LANES]
            out_ref[:, at : at + rows] = block.reshape(parts, rows, LANES)
    power = jnp.broadcast_to(power, (count, LANES)).reshape(parts, rows, LANES)
    lane = lax.broadcasted_iota(jnp.int32, (parts, rows // 2, LANES), 2)
    power = jnp.where(lane == 0, power[:, : rows // 2], power[:, rows // 2 :])
    at = steps * (tile // LANES) * rows
    out_ref[:, at:] = power.astype(jnp.int32).astype(jnp.int16)


def forward(core, own_tab, other_tab, vecs, own, other):
    steps, _, tile, _ = own.shape
    rows, _, part, width = vecs.shape
    count = rows * part
    return pl.pallas_call(
        forward_kernel,
        in_specs=[SMEM] * 3 + [ANY, VMEM] + [ANY] * PIECES,
        out_specs=VMEM,
        out_shape=jax.ShapeDtypeStruct(
            (rows, steps * (tile // LANES) * part + part // 2, LANES), jnp.int16
        ),
        scratch_shapes=[
            pltpu.VMEM((2, rows, part, width), BF16),
            pltpu.VMEM((2 * width // tile + 1, count, tile), BF16),
            pltpu.VMEM((steps, count, tile), F32),
            pltpu.VMEM(own.shape, BF16),
            pltpu.SemaphoreType.DMA((PIECES + 2,)),
        ],
        compiler_params=params(),
        cost_estimate=cost(own, 2 * count),
    )(core, own_tab, other_tab, vecs, own, *other)


def dense_kernel(own_tab, other_tab, own_ref, *refs):
    other_refs, out_ref = refs[:PIECES], refs[PIECES]
    step = pl.program_id(0)
    piece = step // (pl.num_programs(0) // PIECES)
    slots = own_ref.shape[1]
    cols = out_ref.shape[0] // 2
    for side, (tab, sources) in enumerate(((own_tab, [own_ref]), (other_tab, other_refs))):
        for col in range(cols):
            slot = jnp.int32(-1)
            for s in range(slots):
                slot = jnp.where(tab[step, s] == col, s, slot)
            block = jnp.zeros(out_ref.shape[1:], BF16)
            for k, ref in enumerate(sources):
                chosen = slot >= 0 if len(sources) == 1 else (slot >= 0) & (piece == k)
                block = jnp.where(chosen, ref[0, jnp.maximum(slot, 0)], block)
            out_ref[side * cols + col] = block


def dense(own_tab, other_tab, own, other, cols):
    steps, slots, tile, _ = own.shape
    depth = steps // PIECES
    tiles = [pl.BlockSpec((1, slots, tile, tile), lambda t: (t, 0, 0, 0))]
    for k in range(PIECES):
        place = lambda t, k=k: (jnp.clip(t - k * depth, 0, depth - 1), 0, 0, 0)
        tiles.append(pl.BlockSpec((1, slots, tile, tile), place))
    return pl.pallas_call(
        dense_kernel,
        grid=(steps,),
        in_specs=[SMEM, SMEM, *tiles],
        out_specs=pl.BlockSpec((2 * cols, tile, tile), lambda t: (0, t, 0)),
        out_shape=jax.ShapeDtypeStruct((2 * cols, steps * tile, tile), BF16),
        compiler_params=params(),
        cost_estimate=pl.CostEstimate(flops=0, bytes_accessed=8 * own.size, transcendentals=0),
    )(own_tab, other_tab, own, *other)


def settle_kernel(code_ref, out_ref):
    copies, rows, width = out_ref.shape
    groups = width // LANES
    units = []
    for k in range(code_ref.shape[0]):
        power = code_ref[k, groups * rows :].astype(jnp.int32).astype(F32)
        power = jnp.concatenate([power[:, :1], power[:, 1:2]], axis=0)
        units.append(jnp.exp2(power - UNIT_BITS))
    for group in range(groups):
        total = None
        for k, unit in enumerate(units):
            code = code_ref[k, group * rows : (group + 1) * rows]
            term = code.astype(jnp.int32).astype(F32) * unit
            total = term if total is None else total + term
        value = total.astype(BF16)
        for k in range(copies):
            out_ref[k, :, group * LANES : (group + 1) * LANES] = value


def settle(codes, part):
    copies, height, _ = codes.shape
    width = height // part * LANES
    return pl.pallas_call(
        settle_kernel,
        in_specs=[VMEM],
        out_specs=VMEM,
        out_shape=jax.ShapeDtypeStruct((copies, part, width), BF16),
        compiler_params=params(),
    )(codes)


def backward_kernel(core_ref, row_ref, factor_ref, out_ref):
    rows, _, part, _ = out_ref.shape
    cols, _, tile = factor_ref.shape
    core = core_ref[0]
    values = row_ref[...].reshape(rows * part, row_ref.shape[2])
    for col in range(cols):
        place = core if col < cols // 2 else 1 - core
        lo = col % (cols // 2) * tile
        block = jnp.dot(values, factor_ref[col], preferred_element_type=F32)
        out_ref[:, place, :, lo : lo + tile] = block.astype(BF16).reshape(rows, part, tile)


def backward(core, rowvals, factor, shape):
    return pl.pallas_call(
        backward_kernel,
        in_specs=[SMEM, VMEM, VMEM],
        out_specs=VMEM,
        out_shape=jax.ShapeDtypeStruct(shape, BF16),
        compiler_params=params(),
        cost_estimate=cost(factor, rowvals.shape[0] * rowvals.shape[1]),
    )(core, rowvals, factor)


def per_device(n_row, n_col, vectors, factor_tiles, tile_columns, live_counts):
    part = vectors.shape[0] // 2
    width = vectors.shape[1]
    col_tiles = width // factor_tiles.shape[2]
    chips = n_col // 2
    pairs = [(c, c ^ 1) for c in range(n_col)]
    same_core = [[core + 2 * p for p in range(chips)] for core in range(2)]
    row_core = [
        [r * n_col + 2 * p + core for r in range(n_row) for core in range(2)] for p in range(chips)
    ]

    col = lax.axis_index("col")
    core = (col & 1).reshape(1)
    copies = spread(vectors, n_row).reshape(2 * n_row, part, width)
    gathered = swapped(copies, row_core, ("row", "col")).reshape(n_row, 2, part, width)

    slot_index = lax.broadcasted_iota(jnp.int32, tile_columns.shape, 1)
    own_tab = jnp.where(slot_index < live_counts, tile_columns - col * col_tiles, -1)
    other_tab = lax.ppermute(own_tab, "col", pairs)
    other_tiles = []
    for piece in jnp.split(factor_tiles, PIECES):
        piece, other_tab = lax.optimization_barrier((piece, other_tab))
        other_tiles.append(lax.ppermute(piece, "col", pairs))

    factor = dense(own_tab, other_tab, factor_tiles, other_tiles, col_tiles)
    gathered, factor = lax.optimization_barrier((gathered, factor))
    codes = forward(core, own_tab, other_tab, gathered, factor_tiles, other_tiles)
    rowvals = settle(swapped(codes, same_core, "col"), part)
    rowvals = swapped(rowvals, same_core, "col")

    sums = backward(core, rowvals, factor, gathered.shape)
    sums = swapped(sums.reshape(2 * n_row, part, width), row_core, ("row", "col"))
    return sums.reshape(n_row, 2 * part, width).astype(F32).sum(axis=0)


def solution(mesh):
    in_specs = (P("row", "col"), P("row", "col", None, None), P("row", "col"), P("row", "col"))
    body = functools.partial(per_device, mesh.shape["row"], mesh.shape["col"])
    return jax.shard_map(
        body, mesh=mesh, in_specs=in_specs, out_specs=P("row", "col"), check_vma=False
    )
```

```python
import functools

import jax
import jax.numpy as jnp
from jax import lax
from jax.experimental import pallas as pl
from jax.experimental.pallas import tpu as pltpu
from jax.sharding import PartitionSpec as P

BF16, F32 = jnp.bfloat16, jnp.float32
VMEM_BYTES = 24 * 1024 * 1024
LANES = 128
UNIT_BITS = 14
PIECES = 2
ROW_ORDER = (14, 10, 8, 15, 9, 4, 13, 11, 12, 1, 0, 3, 2, 6, 5, 7)
CHIP_ORDER = (3, 14, 7, 9, 13, 11, 4, 5, 12, 8, 1, 0, 15, 6, 2, 10)


def swapped(shard, groups, axes):
    return lax.all_to_all(
        shard, axes, split_axis=0, concat_axis=0, axis_index_groups=groups, tiled=True
    )


SMEM = pl.BlockSpec(memory_space=pltpu.SMEM)
VMEM = pl.BlockSpec(memory_space=pltpu.VMEM)
ANY = pl.BlockSpec(memory_space=pl.ANY)


def params():
    return pltpu.CompilerParams(vmem_limit_bytes=VMEM_BYTES)


def cost(factor, count):
    return pl.CostEstimate(
        flops=2 * factor.size * count, bytes_accessed=2 * factor.size, transcendentals=0
    )


def spread_kernel(vec_ref, out_ref):
    for copy in range(out_ref.shape[0]):
        out_ref[copy] = vec_ref[...]


def spread(vectors, copies):
    return pl.pallas_call(
        spread_kernel,
        in_specs=[VMEM],
        out_specs=VMEM,
        out_shape=jax.ShapeDtypeStruct((copies, *vectors.shape), vectors.dtype),
        compiler_params=params(),
    )(vectors)


def fetches(sources, held, sems):
    depth = sources[0].shape[0]
    return [
        pltpu.make_async_copy(ref, held.at[k * depth : (k + 1) * depth], sems.at[k])
        for k, ref in enumerate(sources)
    ]


def forward_kernel(core_ref, own_tab, other_tab, vec_source, own_ref, *refs):
    sources, (out_ref, vec_ref, picked, total, other_ref, sems) = refs[:PIECES], refs[PIECES:]
    steps, count, tile = total.shape
    per_core = (picked.shape[0] - 1) // 2
    core = core_ref[0]
    copies = [
        pltpu.make_async_copy(vec_source.at[:, side], vec_ref.at[k], sems.at[PIECES + k])
        for k, side in enumerate((core, 1 - core))
    ] + fetches(sources, other_ref, sems)
    for copy in copies:
        copy.start()
    picked[2 * per_core] = jnp.zeros((count, tile), BF16)

    most = jnp.zeros((count, tile), F32)
    for side, (tab, ref) in enumerate(((own_tab, own_ref), (other_tab, other_ref))):
        for copy in copies[1:] if side else copies[:1]:
            copy.wait()
        for col in range(per_core):
            block = vec_ref[side, :, :, col * tile : (col + 1) * tile]
            picked[side * per_core + col] = block.reshape(count, tile)
        for step in range(steps):
            acc = total[step] if side else None
            for slot in range(ref.shape[1]):
                col = tab[step, slot]
                values = picked[jnp.where(col >= 0, side * per_core + col, 2 * per_core)]
                term = lax.dot_general(
                    values, ref[step, slot], (((1,), (1,)), ((), ())), preferred_element_type=F32
                )
                acc = term if acc is None else acc + term
            total[step] = acc
            if side:
                most = jnp.maximum(most, jnp.abs(acc))

    most = jnp.max(most, axis=1, keepdims=True)
    power = jnp.floor(jnp.log2(jnp.maximum(most, 1e-30))) + 1.0
    unit = jnp.exp2(UNIT_BITS - power)
    parts = out_ref.shape[0]
    rows = count // parts
    for step in range(steps):
        code = jnp.floor(total[step] * unit + 0.5).astype(jnp.int32).astype(jnp.int16)
        for half in range(tile // LANES):
            at = (step * (tile // LANES) + half) * rows
            block = code[:, half * LANES : (half + 1) * LANES]
            out_ref[:, at : at + rows] = block.reshape(parts, rows, LANES)
    power = jnp.broadcast_to(power, (count, LANES)).reshape(parts, rows, LANES)
    lane = lax.broadcasted_iota(jnp.int32, (parts, rows // 2, LANES), 2)
    power = jnp.where(lane == 0, power[:, : rows // 2], power[:, rows // 2 :])
    at = steps * (tile // LANES) * rows
    out_ref[:, at:] = power.astype(jnp.int32).astype(jnp.int16)


def forward(core, own_tab, other_tab, vecs, own, other):
    steps, _, tile, _ = own.shape
    rows, _, part, width = vecs.shape
    count = rows * part
    return pl.pallas_call(
        forward_kernel,
        in_specs=[SMEM] * 3 + [ANY, VMEM] + [ANY] * PIECES,
        out_specs=VMEM,
        out_shape=jax.ShapeDtypeStruct(
            (rows, steps * (tile // LANES) * part + part // 2, LANES), jnp.int16
        ),
        scratch_shapes=[
            pltpu.VMEM((2, rows, part, width), BF16),
            pltpu.VMEM((2 * width // tile + 1, count, tile), BF16),
            pltpu.VMEM((steps, count, tile), F32),
            pltpu.VMEM(own.shape, BF16),
            pltpu.SemaphoreType.DMA((PIECES + 2,)),
        ],
        compiler_params=params(),
        cost_estimate=cost(own, 2 * count),
    )(core, own_tab, other_tab, vecs, own, *other)


def dense_kernel(own_tab, other_tab, own_ref, *refs):
    other_refs, out_ref = refs[:PIECES], refs[PIECES]
    step = pl.program_id(0)
    piece = step // (pl.num_programs(0) // PIECES)
    slots = own_ref.shape[1]
    cols = out_ref.shape[0] // 2
    for side, (tab, sources) in enumerate(((own_tab, [own_ref]), (other_tab, other_refs))):
        for col in range(cols):
            slot = jnp.int32(-1)
            for s in range(slots):
                slot = jnp.where(tab[step, s] == col, s, slot)
            block = jnp.zeros(out_ref.shape[1:], BF16)
            for k, ref in enumerate(sources):
                chosen = slot >= 0 if len(sources) == 1 else (slot >= 0) & (piece == k)
                block = jnp.where(chosen, ref[0, jnp.maximum(slot, 0)], block)
            out_ref[side * cols + col] = block


def dense(own_tab, other_tab, own, other, cols):
    steps, slots, tile, _ = own.shape
    depth = steps // PIECES
    tiles = [pl.BlockSpec((1, slots, tile, tile), lambda t: (t, 0, 0, 0))]
    for k in range(PIECES):
        place = lambda t, k=k: (jnp.clip(t - k * depth, 0, depth - 1), 0, 0, 0)
        tiles.append(pl.BlockSpec((1, slots, tile, tile), place))
    return pl.pallas_call(
        dense_kernel,
        grid=(steps,),
        in_specs=[SMEM, SMEM, *tiles],
        out_specs=pl.BlockSpec((2 * cols, tile, tile), lambda t: (0, t, 0)),
        out_shape=jax.ShapeDtypeStruct((2 * cols, steps * tile, tile), BF16),
        compiler_params=params(),
        cost_estimate=pl.CostEstimate(flops=0, bytes_accessed=8 * own.size, transcendentals=0),
    )(own_tab, other_tab, own, *other)


def settle_kernel(code_ref, out_ref):
    copies, rows, width = out_ref.shape
    groups = width // LANES
    units = []
    for k in range(code_ref.shape[0]):
        power = code_ref[k, groups * rows :].astype(jnp.int32).astype(F32)
        power = jnp.concatenate([power[:, :1], power[:, 1:2]], axis=0)
        units.append(jnp.exp2(power - UNIT_BITS))
    for group in range(groups):
        total = None
        for k, unit in enumerate(units):
            code = code_ref[k, group * rows : (group + 1) * rows]
            term = code.astype(jnp.int32).astype(F32) * unit
            total = term if total is None else total + term
        value = total.astype(BF16)
        for k in range(copies):
            out_ref[k, :, group * LANES : (group + 1) * LANES] = value


def settle(codes, part):
    copies, height, _ = codes.shape
    width = height // part * LANES
    return pl.pallas_call(
        settle_kernel,
        in_specs=[VMEM],
        out_specs=VMEM,
        out_shape=jax.ShapeDtypeStruct((copies, part, width), BF16),
        compiler_params=params(),
    )(codes)


def backward_kernel(core_ref, row_ref, factor_ref, out_ref):
    rows, _, part, _ = out_ref.shape
    cols, _, tile = factor_ref.shape
    core = core_ref[0]
    values = row_ref[...].reshape(rows * part, row_ref.shape[2])
    for col in range(cols):
        place = core if col < cols // 2 else 1 - core
        lo = col % (cols // 2) * tile
        block = jnp.dot(values, factor_ref[col], preferred_element_type=F32)
        out_ref[:, place, :, lo : lo + tile] = block.astype(BF16).reshape(rows, part, tile)


def backward(core, rowvals, factor, shape):
    return pl.pallas_call(
        backward_kernel,
        in_specs=[SMEM, VMEM, VMEM],
        out_specs=VMEM,
        out_shape=jax.ShapeDtypeStruct(shape, BF16),
        compiler_params=params(),
        cost_estimate=cost(factor, rowvals.shape[0] * rowvals.shape[1]),
    )(core, rowvals, factor)


def per_device(n_row, n_col, vectors, factor_tiles, tile_columns, live_counts):
    part = vectors.shape[0] // 2
    width = vectors.shape[1]
    col_tiles = width // factor_tiles.shape[2]
    chips = n_col // 2
    pairs = [(c, c ^ 1) for c in range(n_col)]
    same_core = [[core + 2 * p for p in CHIP_ORDER] for core in range(2)]
    row_core = [
        [r * n_col + 2 * p + core for r in ROW_ORDER for core in range(2)] for p in range(chips)
    ]

    col = lax.axis_index("col")
    core = (col & 1).reshape(1)
    copies = spread(vectors, n_row).reshape(2 * n_row, part, width)
    gathered = swapped(copies, row_core, ("row", "col")).reshape(n_row, 2, part, width)

    slot_index = lax.broadcasted_iota(jnp.int32, tile_columns.shape, 1)
    own_tab = jnp.where(slot_index < live_counts, tile_columns - col * col_tiles, -1)
    other_tab = lax.ppermute(own_tab, "col", pairs)
    other_tiles = []
    for piece in jnp.split(factor_tiles, PIECES):
        piece, other_tab = lax.optimization_barrier((piece, other_tab))
        other_tiles.append(lax.ppermute(piece, "col", pairs))

    factor = dense(own_tab, other_tab, factor_tiles, other_tiles, col_tiles)
    gathered, factor = lax.optimization_barrier((gathered, factor))
    codes = forward(core, own_tab, other_tab, gathered, factor_tiles, other_tiles)
    rowvals = settle(swapped(codes, same_core, "col"), part)
    rowvals = swapped(rowvals, same_core, "col")

    sums = backward(core, rowvals, factor, gathered.shape)
    sums = swapped(sums.reshape(2 * n_row, part, width), row_core, ("row", "col"))
    return sums.reshape(n_row, 2 * part, width).astype(F32).sum(axis=0)


def solution(mesh):
    in_specs = (P("row", "col"), P("row", "col", None, None), P("row", "col"), P("row", "col"))
    body = functools.partial(per_device, mesh.shape["row"], mesh.shape["col"])
    return jax.shard_map(
        body, mesh=mesh, in_specs=in_specs, out_specs=P("row", "col"), check_vma=False
    )
```

```python
import functools

import jax
import jax.numpy as jnp
from jax import lax
from jax.experimental import pallas as pl
from jax.experimental.pallas import tpu as pltpu
from jax.sharding import PartitionSpec as P

BF16, F32 = jnp.bfloat16, jnp.float32
VMEM_BYTES = 24 * 1024 * 1024
LANES = 128
UNIT_BITS = 14
PIECES = 2
ROW_ORDER = (14, 10, 8, 15, 9, 4, 13, 11, 12, 1, 0, 3, 2, 6, 5, 7)
CHIP_ORDERS = ((6, 15, 14, 8, 13, 10, 11, 12, 5, 1, 2, 7, 9, 0, 3, 4), (11, 5, 3, 7, 12, 2, 10, 8, 6, 4, 15, 0, 1, 13, 14, 9))


def swapped(shard, groups, axes):
    return lax.all_to_all(
        shard, axes, split_axis=0, concat_axis=0, axis_index_groups=groups, tiled=True
    )


SMEM = pl.BlockSpec(memory_space=pltpu.SMEM)
VMEM = pl.BlockSpec(memory_space=pltpu.VMEM)
ANY = pl.BlockSpec(memory_space=pl.ANY)


def params():
    return pltpu.CompilerParams(vmem_limit_bytes=VMEM_BYTES)


def cost(factor, count):
    return pl.CostEstimate(
        flops=2 * factor.size * count, bytes_accessed=2 * factor.size, transcendentals=0
    )


def spread_kernel(vec_ref, out_ref):
    for copy in range(out_ref.shape[0]):
        out_ref[copy] = vec_ref[...]


def spread(vectors, copies):
    return pl.pallas_call(
        spread_kernel,
        in_specs=[VMEM],
        out_specs=VMEM,
        out_shape=jax.ShapeDtypeStruct((copies, *vectors.shape), vectors.dtype),
        compiler_params=params(),
    )(vectors)


def fetches(sources, held, sems):
    depth = sources[0].shape[0]
    return [
        pltpu.make_async_copy(ref, held.at[k * depth : (k + 1) * depth], sems.at[k])
        for k, ref in enumerate(sources)
    ]


def forward_kernel(core_ref, own_tab, other_tab, vec_source, own_ref, *refs):
    sources, (out_ref, vec_ref, picked, total, other_ref, sems) = refs[:PIECES], refs[PIECES:]
    steps, count, tile = total.shape
    per_core = (picked.shape[0] - 1) // 2
    core = core_ref[0]
    copies = [
        pltpu.make_async_copy(vec_source.at[:, side], vec_ref.at[k], sems.at[PIECES + k])
        for k, side in enumerate((core, 1 - core))
    ] + fetches(sources, other_ref, sems)
    for copy in copies:
        copy.start()
    picked[2 * per_core] = jnp.zeros((count, tile), BF16)

    most = jnp.zeros((count, tile), F32)
    for side, (tab, ref) in enumerate(((own_tab, own_ref), (other_tab, other_ref))):
        for copy in copies[1:] if side else copies[:1]:
            copy.wait()
        for col in range(per_core):
            block = vec_ref[side, :, :, col * tile : (col + 1) * tile]
            picked[side * per_core + col] = block.reshape(count, tile)
        for step in range(steps):
            acc = total[step] if side else None
            for slot in range(ref.shape[1]):
                col = tab[step, slot]
                values = picked[jnp.where(col >= 0, side * per_core + col, 2 * per_core)]
                term = lax.dot_general(
                    values, ref[step, slot], (((1,), (1,)), ((), ())), preferred_element_type=F32
                )
                acc = term if acc is None else acc + term
            total[step] = acc
            if side:
                most = jnp.maximum(most, jnp.abs(acc))

    most = jnp.max(most, axis=1, keepdims=True)
    power = jnp.floor(jnp.log2(jnp.maximum(most, 1e-30))) + 1.0
    unit = jnp.exp2(UNIT_BITS - power)
    parts = out_ref.shape[0]
    rows = count // parts
    for step in range(steps):
        code = jnp.floor(total[step] * unit + 0.5).astype(jnp.int32).astype(jnp.int16)
        for half in range(tile // LANES):
            at = (step * (tile // LANES) + half) * rows
            block = code[:, half * LANES : (half + 1) * LANES]
            out_ref[:, at : at + rows] = block.reshape(parts, rows, LANES)
    power = jnp.broadcast_to(power, (count, LANES)).reshape(parts, rows, LANES)
    lane = lax.broadcasted_iota(jnp.int32, (parts, rows // 2, LANES), 2)
    power = jnp.where(lane == 0, power[:, : rows // 2], power[:, rows // 2 :])
    at = steps * (tile // LANES) * rows
    out_ref[:, at:] = power.astype(jnp.int32).astype(jnp.int16)


def forward(core, own_tab, other_tab, vecs, own, other):
    steps, _, tile, _ = own.shape
    rows, _, part, width = vecs.shape
    count = rows * part
    return pl.pallas_call(
        forward_kernel,
        in_specs=[SMEM] * 3 + [ANY, VMEM] + [ANY] * PIECES,
        out_specs=VMEM,
        out_shape=jax.ShapeDtypeStruct(
            (rows, steps * (tile // LANES) * part + part // 2, LANES), jnp.int16
        ),
        scratch_shapes=[
            pltpu.VMEM((2, rows, part, width), BF16),
            pltpu.VMEM((2 * width // tile + 1, count, tile), BF16),
            pltpu.VMEM((steps, count, tile), F32),
            pltpu.VMEM(own.shape, BF16),
            pltpu.SemaphoreType.DMA((PIECES + 2,)),
        ],
        compiler_params=params(),
        cost_estimate=cost(own, 2 * count),
    )(core, own_tab, other_tab, vecs, own, *other)


def dense_kernel(own_tab, other_tab, own_ref, *refs):
    other_refs, out_ref = refs[:PIECES], refs[PIECES]
    step = pl.program_id(0)
    piece = step // (pl.num_programs(0) // PIECES)
    slots = own_ref.shape[1]
    cols = out_ref.shape[0] // 2
    for side, (tab, sources) in enumerate(((own_tab, [own_ref]), (other_tab, other_refs))):
        for col in range(cols):
            slot = jnp.int32(-1)
            for s in range(slots):
                slot = jnp.where(tab[step, s] == col, s, slot)
            block = jnp.zeros(out_ref.shape[1:], BF16)
            for k, ref in enumerate(sources):
                chosen = slot >= 0 if len(sources) == 1 else (slot >= 0) & (piece == k)
                block = jnp.where(chosen, ref[0, jnp.maximum(slot, 0)], block)
            out_ref[side * cols + col] = block


def dense(own_tab, other_tab, own, other, cols):
    steps, slots, tile, _ = own.shape
    depth = steps // PIECES
    tiles = [pl.BlockSpec((1, slots, tile, tile), lambda t: (t, 0, 0, 0))]
    for k in range(PIECES):
        place = lambda t, k=k: (jnp.clip(t - k * depth, 0, depth - 1), 0, 0, 0)
        tiles.append(pl.BlockSpec((1, slots, tile, tile), place))
    return pl.pallas_call(
        dense_kernel,
        grid=(steps,),
        in_specs=[SMEM, SMEM, *tiles],
        out_specs=pl.BlockSpec((2 * cols, tile, tile), lambda t: (0, t, 0)),
        out_shape=jax.ShapeDtypeStruct((2 * cols, steps * tile, tile), BF16),
        compiler_params=params(),
        cost_estimate=pl.CostEstimate(flops=0, bytes_accessed=8 * own.size, transcendentals=0),
    )(own_tab, other_tab, own, *other)


def settle_kernel(code_ref, out_ref):
    copies, rows, width = out_ref.shape
    groups = width // LANES
    units = []
    for k in range(code_ref.shape[0]):
        power = code_ref[k, groups * rows :].astype(jnp.int32).astype(F32)
        power = jnp.concatenate([power[:, :1], power[:, 1:2]], axis=0)
        units.append(jnp.exp2(power - UNIT_BITS))
    for group in range(groups):
        total = None
        for k, unit in enumerate(units):
            code = code_ref[k, group * rows : (group + 1) * rows]
            term = code.astype(jnp.int32).astype(F32) * unit
            total = term if total is None else total + term
        value = total.astype(BF16)
        for k in range(copies):
            out_ref[k, :, group * LANES : (group + 1) * LANES] = value


def settle(codes, part):
    copies, height, _ = codes.shape
    width = height // part * LANES
    return pl.pallas_call(
        settle_kernel,
        in_specs=[VMEM],
        out_specs=VMEM,
        out_shape=jax.ShapeDtypeStruct((copies, part, width), BF16),
        compiler_params=params(),
    )(codes)


def backward_kernel(core_ref, row_ref, factor_ref, out_ref):
    rows, _, part, _ = out_ref.shape
    cols, _, tile = factor_ref.shape
    core = core_ref[0]
    values = row_ref[...].reshape(rows * part, row_ref.shape[2])
    for col in range(cols):
        place = core if col < cols // 2 else 1 - core
        lo = col % (cols // 2) * tile
        block = jnp.dot(values, factor_ref[col], preferred_element_type=F32)
        out_ref[:, place, :, lo : lo + tile] = block.astype(BF16).reshape(rows, part, tile)


def backward(core, rowvals, factor, shape):
    return pl.pallas_call(
        backward_kernel,
        in_specs=[SMEM, VMEM, VMEM],
        out_specs=VMEM,
        out_shape=jax.ShapeDtypeStruct(shape, BF16),
        compiler_params=params(),
        cost_estimate=cost(factor, rowvals.shape[0] * rowvals.shape[1]),
    )(core, rowvals, factor)


def row_sum_kernel(part_ref, out_ref):
    total = part_ref[0].astype(F32)
    for k in range(1, part_ref.shape[0]):
        total = total + part_ref[k].astype(F32)
    out_ref[...] = total


def row_sum(parts):
    return pl.pallas_call(
        row_sum_kernel,
        in_specs=[VMEM],
        out_specs=VMEM,
        out_shape=jax.ShapeDtypeStruct(parts.shape[1:], F32),
        compiler_params=params(),
    )(parts)


def per_device(n_row, n_col, vectors, factor_tiles, tile_columns, live_counts):
    part = vectors.shape[0] // 2
    width = vectors.shape[1]
    col_tiles = width // factor_tiles.shape[2]
    chips = n_col // 2
    pairs = [(c, c ^ 1) for c in range(n_col)]
    same_core = [[core + 2 * p for p in CHIP_ORDERS[core]] for core in range(2)]
    row_core = [
        [r * n_col + 2 * p + core for r in ROW_ORDER for core in range(2)] for p in range(chips)
    ]

    col = lax.axis_index("col")
    core = (col & 1).reshape(1)
    copies = spread(vectors, n_row).reshape(2 * n_row, part, width)
    gathered = swapped(copies, row_core, ("row", "col")).reshape(n_row, 2, part, width)

    slot_index = lax.broadcasted_iota(jnp.int32, tile_columns.shape, 1)
    own_tab = jnp.where(slot_index < live_counts, tile_columns - col * col_tiles, -1)
    other_tab = lax.ppermute(own_tab, "col", pairs)
    other_tiles = []
    for piece in jnp.split(factor_tiles, PIECES):
        piece, other_tab = lax.optimization_barrier((piece, other_tab))
        other_tiles.append(lax.ppermute(piece, "col", pairs))

    factor = dense(own_tab, other_tab, factor_tiles, other_tiles, col_tiles)
    gathered, factor = lax.optimization_barrier((gathered, factor))
    codes = forward(core, own_tab, other_tab, gathered, factor_tiles, other_tiles)
    rowvals = settle(swapped(codes, same_core, "col"), part)
    rowvals = swapped(rowvals, same_core, "col")

    sums = backward(core, rowvals, factor, gathered.shape)
    sums = swapped(sums.reshape(2 * n_row, part, width), row_core, ("row", "col"))
    return row_sum(sums.reshape(n_row, 2 * part, width))


def solution(mesh):
    in_specs = (P("row", "col"), P("row", "col", None, None), P("row", "col"), P("row", "col"))
    body = functools.partial(per_device, mesh.shape["row"], mesh.shape["col"])
    return jax.shard_map(
        body, mesh=mesh, in_specs=in_specs, out_specs=P("row", "col"), check_vma=False
    )
```

```python
import functools

import jax
import jax.numpy as jnp
from jax import lax
from jax.experimental import pallas as pl
from jax.experimental.pallas import tpu as pltpu
from jax.sharding import PartitionSpec as P

BF16, F32 = jnp.bfloat16, jnp.float32
VMEM_BYTES = 24 * 1024 * 1024
LANES = 128
UNIT_BITS = 14
PIECES = 2
ROW_ORDER = (14, 10, 8, 15, 9, 4, 13, 11, 12, 1, 0, 3, 2, 6, 5, 7)
CHIP_ORDERS = ((3, 14, 7, 9, 13, 11, 4, 5, 12, 8, 1, 0, 15, 6, 2, 10), (14, 10, 8, 15, 9, 4, 13, 11, 12, 1, 0, 3, 2, 6, 5, 7))


def swapped(shard, groups, axes):
    return lax.all_to_all(
        shard, axes, split_axis=0, concat_axis=0, axis_index_groups=groups, tiled=True
    )


SMEM = pl.BlockSpec(memory_space=pltpu.SMEM)
VMEM = pl.BlockSpec(memory_space=pltpu.VMEM)
ANY = pl.BlockSpec(memory_space=pl.ANY)


def params():
    return pltpu.CompilerParams(vmem_limit_bytes=VMEM_BYTES)


def cost(factor, count):
    return pl.CostEstimate(
        flops=2 * factor.size * count, bytes_accessed=2 * factor.size, transcendentals=0
    )


def spread_kernel(vec_ref, out_ref):
    for copy in range(out_ref.shape[0]):
        out_ref[copy] = vec_ref[...]


def spread(vectors, copies):
    return pl.pallas_call(
        spread_kernel,
        in_specs=[VMEM],
        out_specs=VMEM,
        out_shape=jax.ShapeDtypeStruct((copies, *vectors.shape), vectors.dtype),
        compiler_params=params(),
    )(vectors)


def fetches(sources, held, sems):
    depth = sources[0].shape[0]
    return [
        pltpu.make_async_copy(ref, held.at[k * depth : (k + 1) * depth], sems.at[k])
        for k, ref in enumerate(sources)
    ]


def forward_kernel(core_ref, own_tab, other_tab, vec_source, own_ref, *refs):
    sources, (out_ref, vec_ref, picked, total, other_ref, sems) = refs[:PIECES], refs[PIECES:]
    steps, count, tile = total.shape
    per_core = (picked.shape[0] - 1) // 2
    core = core_ref[0]
    copies = [
        pltpu.make_async_copy(vec_source.at[:, side], vec_ref.at[k], sems.at[PIECES + k])
        for k, side in enumerate((core, 1 - core))
    ] + fetches(sources, other_ref, sems)
    for copy in copies:
        copy.start()
    picked[2 * per_core] = jnp.zeros((count, tile), BF16)

    most = jnp.zeros((count, tile), F32)
    for side, (tab, ref) in enumerate(((own_tab, own_ref), (other_tab, other_ref))):
        for copy in copies[1:] if side else copies[:1]:
            copy.wait()
        for col in range(per_core):
            block = vec_ref[side, :, :, col * tile : (col + 1) * tile]
            picked[side * per_core + col] = block.reshape(count, tile)
        for step in range(steps):
            acc = total[step] if side else None
            for slot in range(ref.shape[1]):
                col = tab[step, slot]
                values = picked[jnp.where(col >= 0, side * per_core + col, 2 * per_core)]
                term = lax.dot_general(
                    values, ref[step, slot], (((1,), (1,)), ((), ())), preferred_element_type=F32
                )
                acc = term if acc is None else acc + term
            total[step] = acc
            if side:
                most = jnp.maximum(most, jnp.abs(acc))

    most = jnp.max(most, axis=1, keepdims=True)
    power = jnp.floor(jnp.log2(jnp.maximum(most, 1e-30))) + 1.0
    unit = jnp.exp2(UNIT_BITS - power)
    parts = out_ref.shape[0]
    rows = count // parts
    for step in range(steps):
        code = jnp.floor(total[step] * unit + 0.5).astype(jnp.int32).astype(jnp.int16)
        for half in range(tile // LANES):
            at = (step * (tile // LANES) + half) * rows
            block = code[:, half * LANES : (half + 1) * LANES]
            out_ref[:, at : at + rows] = block.reshape(parts, rows, LANES)
    power = jnp.broadcast_to(power, (count, LANES)).reshape(parts, rows, LANES)
    lane = lax.broadcasted_iota(jnp.int32, (parts, rows // 2, LANES), 2)
    power = jnp.where(lane == 0, power[:, : rows // 2], power[:, rows // 2 :])
    at = steps * (tile // LANES) * rows
    out_ref[:, at:] = power.astype(jnp.int32).astype(jnp.int16)


def forward(core, own_tab, other_tab, vecs, own, other):
    steps, _, tile, _ = own.shape
    rows, _, part, width = vecs.shape
    count = rows * part
    return pl.pallas_call(
        forward_kernel,
        in_specs=[SMEM] * 3 + [ANY, VMEM] + [ANY] * PIECES,
        out_specs=VMEM,
        out_shape=jax.ShapeDtypeStruct(
            (rows, steps * (tile // LANES) * part + part // 2, LANES), jnp.int16
        ),
        scratch_shapes=[
            pltpu.VMEM((2, rows, part, width), BF16),
            pltpu.VMEM((2 * width // tile + 1, count, tile), BF16),
            pltpu.VMEM((steps, count, tile), F32),
            pltpu.VMEM(own.shape, BF16),
            pltpu.SemaphoreType.DMA((PIECES + 2,)),
        ],
        compiler_params=params(),
        cost_estimate=cost(own, 2 * count),
    )(core, own_tab, other_tab, vecs, own, *other)


def dense_kernel(own_tab, other_tab, own_ref, *refs):
    other_refs, out_ref = refs[:PIECES], refs[PIECES]
    step = pl.program_id(0)
    piece = step // (pl.num_programs(0) // PIECES)
    slots = own_ref.shape[1]
    cols = out_ref.shape[0] // 2
    for side, (tab, sources) in enumerate(((own_tab, [own_ref]), (other_tab, other_refs))):
        for col in range(cols):
            slot = jnp.int32(-1)
            for s in range(slots):
                slot = jnp.where(tab[step, s] == col, s, slot)
            block = jnp.zeros(out_ref.shape[1:], BF16)
            for k, ref in enumerate(sources):
                chosen = slot >= 0 if len(sources) == 1 else (slot >= 0) & (piece == k)
                block = jnp.where(chosen, ref[0, jnp.maximum(slot, 0)], block)
            out_ref[side * cols + col] = block


def dense(own_tab, other_tab, own, other, cols):
    steps, slots, tile, _ = own.shape
    depth = steps // PIECES
    tiles = [pl.BlockSpec((1, slots, tile, tile), lambda t: (t, 0, 0, 0))]
    for k in range(PIECES):
        place = lambda t, k=k: (jnp.clip(t - k * depth, 0, depth - 1), 0, 0, 0)
        tiles.append(pl.BlockSpec((1, slots, tile, tile), place))
    return pl.pallas_call(
        dense_kernel,
        grid=(steps,),
        in_specs=[SMEM, SMEM, *tiles],
        out_specs=pl.BlockSpec((2 * cols, tile, tile), lambda t: (0, t, 0)),
        out_shape=jax.ShapeDtypeStruct((2 * cols, steps * tile, tile), BF16),
        compiler_params=params(),
        cost_estimate=pl.CostEstimate(flops=0, bytes_accessed=8 * own.size, transcendentals=0),
    )(own_tab, other_tab, own, *other)


def settle_kernel(code_ref, out_ref):
    copies, rows, width = out_ref.shape
    groups = width // LANES
    units = []
    for k in range(code_ref.shape[0]):
        power = code_ref[k, groups * rows :].astype(jnp.int32).astype(F32)
        power = jnp.concatenate([power[:, :1], power[:, 1:2]], axis=0)
        units.append(jnp.exp2(power - UNIT_BITS))
    for group in range(groups):
        total = None
        for k, unit in enumerate(units):
            code = code_ref[k, group * rows : (group + 1) * rows]
            term = code.astype(jnp.int32).astype(F32) * unit
            total = term if total is None else total + term
        value = total.astype(BF16)
        for k in range(copies):
            out_ref[k, :, group * LANES : (group + 1) * LANES] = value


def settle(codes, part):
    copies, height, _ = codes.shape
    width = height // part * LANES
    return pl.pallas_call(
        settle_kernel,
        in_specs=[VMEM],
        out_specs=VMEM,
        out_shape=jax.ShapeDtypeStruct((copies, part, width), BF16),
        compiler_params=params(),
    )(codes)


def backward_kernel(core_ref, row_ref, factor_ref, out_ref):
    rows, _, part, _ = out_ref.shape
    cols, _, tile = factor_ref.shape
    core = core_ref[0]
    values = row_ref[...].reshape(rows * part, row_ref.shape[2])
    for col in range(cols):
        place = core if col < cols // 2 else 1 - core
        lo = col % (cols // 2) * tile
        block = jnp.dot(values, factor_ref[col], preferred_element_type=F32)
        out_ref[:, place, :, lo : lo + tile] = block.astype(BF16).reshape(rows, part, tile)


def backward(core, rowvals, factor, shape):
    return pl.pallas_call(
        backward_kernel,
        in_specs=[SMEM, VMEM, VMEM],
        out_specs=VMEM,
        out_shape=jax.ShapeDtypeStruct(shape, BF16),
        compiler_params=params(),
        cost_estimate=cost(factor, rowvals.shape[0] * rowvals.shape[1]),
    )(core, rowvals, factor)


def row_sum_kernel(part_ref, out_ref):
    total = part_ref[0].astype(F32)
    for k in range(1, part_ref.shape[0]):
        total = total + part_ref[k].astype(F32)
    out_ref[...] = total


def row_sum(parts):
    return pl.pallas_call(
        row_sum_kernel,
        in_specs=[VMEM],
        out_specs=VMEM,
        out_shape=jax.ShapeDtypeStruct(parts.shape[1:], F32),
        compiler_params=params(),
    )(parts)


def per_device(n_row, n_col, vectors, factor_tiles, tile_columns, live_counts):
    part = vectors.shape[0] // 2
    width = vectors.shape[1]
    col_tiles = width // factor_tiles.shape[2]
    chips = n_col // 2
    pairs = [(c, c ^ 1) for c in range(n_col)]
    same_core = [[core + 2 * p for p in CHIP_ORDERS[core]] for core in range(2)]
    row_core = [
        [r * n_col + 2 * p + core for r in ROW_ORDER for core in range(2)] for p in range(chips)
    ]

    col = lax.axis_index("col")
    core = (col & 1).reshape(1)
    copies = spread(vectors, n_row).reshape(2 * n_row, part, width)
    gathered = swapped(copies, row_core, ("row", "col")).reshape(n_row, 2, part, width)

    slot_index = lax.broadcasted_iota(jnp.int32, tile_columns.shape, 1)
    own_tab = jnp.where(slot_index < live_counts, tile_columns - col * col_tiles, -1)
    other_tab = lax.ppermute(own_tab, "col", pairs)
    other_tiles = []
    for piece in jnp.split(factor_tiles, PIECES):
        piece, other_tab = lax.optimization_barrier((piece, other_tab))
        other_tiles.append(lax.ppermute(piece, "col", pairs))

    factor = dense(own_tab, other_tab, factor_tiles, other_tiles, col_tiles)
    gathered, factor = lax.optimization_barrier((gathered, factor))
    codes = forward(core, own_tab, other_tab, gathered, factor_tiles, other_tiles)
    rowvals = settle(swapped(codes, same_core, "col"), part)
    rowvals = swapped(rowvals, same_core, "col")

    sums = backward(core, rowvals, factor, gathered.shape)
    sums = swapped(sums.reshape(2 * n_row, part, width), row_core, ("row", "col"))
    return row_sum(sums.reshape(n_row, 2 * part, width))


def solution(mesh):
    in_specs = (P("row", "col"), P("row", "col", None, None), P("row", "col"), P("row", "col"))
    body = functools.partial(per_device, mesh.shape["row"], mesh.shape["col"])
    return jax.shard_map(
        body, mesh=mesh, in_specs=in_specs, out_specs=P("row", "col"), check_vma=False
    )
```

```python
import functools

import jax
import jax.numpy as jnp
from jax import lax
from jax.experimental import pallas as pl
from jax.experimental.pallas import tpu as pltpu
from jax.sharding import PartitionSpec as P

BF16, F32 = jnp.bfloat16, jnp.float32
VMEM_BYTES = 24 * 1024 * 1024
LANES = 128
UNIT_BITS = 14
PIECES = 2
ROW_ORDER = (4, 9, 7, 10, 1, 5, 15, 13, 12, 3, 2, 14, 11, 8, 0, 6)
CHIP_ORDERS = ((3, 14, 7, 9, 13, 11, 4, 5, 12, 8, 1, 0, 15, 6, 2, 10), (14, 10, 8, 15, 9, 4, 13, 11, 12, 1, 0, 3, 2, 6, 5, 7))


def swapped(shard, groups, axes):
    return lax.all_to_all(
        shard, axes, split_axis=0, concat_axis=0, axis_index_groups=groups, tiled=True
    )


SMEM = pl.BlockSpec(memory_space=pltpu.SMEM)
VMEM = pl.BlockSpec(memory_space=pltpu.VMEM)
ANY = pl.BlockSpec(memory_space=pl.ANY)


def params():
    return pltpu.CompilerParams(vmem_limit_bytes=VMEM_BYTES)


def cost(factor, count):
    return pl.CostEstimate(
        flops=2 * factor.size * count, bytes_accessed=2 * factor.size, transcendentals=0
    )


def spread_kernel(vec_ref, out_ref):
    for copy in range(out_ref.shape[0]):
        out_ref[copy] = vec_ref[...]


def spread(vectors, copies):
    return pl.pallas_call(
        spread_kernel,
        in_specs=[VMEM],
        out_specs=VMEM,
        out_shape=jax.ShapeDtypeStruct((copies, *vectors.shape), vectors.dtype),
        compiler_params=params(),
    )(vectors)


def fetches(sources, held, sems):
    depth = sources[0].shape[0]
    return [
        pltpu.make_async_copy(ref, held.at[k * depth : (k + 1) * depth], sems.at[k])
        for k, ref in enumerate(sources)
    ]


def forward_kernel(core_ref, own_tab, other_tab, vec_source, own_ref, *refs):
    sources, (out_ref, vec_ref, picked, total, other_ref, sems) = refs[:PIECES], refs[PIECES:]
    steps, count, tile = total.shape
    per_core = (picked.shape[0] - 1) // 2
    core = core_ref[0]
    copies = [
        pltpu.make_async_copy(vec_source.at[:, side], vec_ref.at[k], sems.at[PIECES + k])
        for k, side in enumerate((core, 1 - core))
    ] + fetches(sources, other_ref, sems)
    for copy in copies:
        copy.start()
    picked[2 * per_core] = jnp.zeros((count, tile), BF16)

    most = jnp.zeros((count, tile), F32)
    for side, (tab, ref) in enumerate(((own_tab, own_ref), (other_tab, other_ref))):
        for copy in copies[1:] if side else copies[:1]:
            copy.wait()
        for col in range(per_core):
            block = vec_ref[side, :, :, col * tile : (col + 1) * tile]
            picked[side * per_core + col] = block.reshape(count, tile)
        for step in range(steps):
            acc = total[step] if side else None
            for slot in range(ref.shape[1]):
                col = tab[step, slot]
                values = picked[jnp.where(col >= 0, side * per_core + col, 2 * per_core)]
                term = lax.dot_general(
                    values, ref[step, slot], (((1,), (1,)), ((), ())), preferred_element_type=F32
                )
                acc = term if acc is None else acc + term
            total[step] = acc
            if side:
                most = jnp.maximum(most, jnp.abs(acc))

    most = jnp.max(most, axis=1, keepdims=True)
    power = jnp.floor(jnp.log2(jnp.maximum(most, 1e-30))) + 1.0
    unit = jnp.exp2(UNIT_BITS - power)
    parts = out_ref.shape[0]
    rows = count // parts
    for step in range(steps):
        code = jnp.floor(total[step] * unit + 0.5).astype(jnp.int32).astype(jnp.int16)
        for half in range(tile // LANES):
            at = (step * (tile // LANES) + half) * rows
            block = code[:, half * LANES : (half + 1) * LANES]
            out_ref[:, at : at + rows] = block.reshape(parts, rows, LANES)
    power = jnp.broadcast_to(power, (count, LANES)).reshape(parts, rows, LANES)
    lane = lax.broadcasted_iota(jnp.int32, (parts, rows // 2, LANES), 2)
    power = jnp.where(lane == 0, power[:, : rows // 2], power[:, rows // 2 :])
    at = steps * (tile // LANES) * rows
    out_ref[:, at:] = power.astype(jnp.int32).astype(jnp.int16)


def forward(core, own_tab, other_tab, vecs, own, other):
    steps, _, tile, _ = own.shape
    rows, _, part, width = vecs.shape
    count = rows * part
    return pl.pallas_call(
        forward_kernel,
        in_specs=[SMEM] * 3 + [ANY, VMEM] + [ANY] * PIECES,
        out_specs=VMEM,
        out_shape=jax.ShapeDtypeStruct(
            (rows, steps * (tile // LANES) * part + part // 2, LANES), jnp.int16
        ),
        scratch_shapes=[
            pltpu.VMEM((2, rows, part, width), BF16),
            pltpu.VMEM((2 * width // tile + 1, count, tile), BF16),
            pltpu.VMEM((steps, count, tile), F32),
            pltpu.VMEM(own.shape, BF16),
            pltpu.SemaphoreType.DMA((PIECES + 2,)),
        ],
        compiler_params=params(),
        cost_estimate=cost(own, 2 * count),
    )(core, own_tab, other_tab, vecs, own, *other)


def dense_kernel(own_tab, other_tab, own_ref, *refs):
    other_refs, out_ref = refs[:PIECES], refs[PIECES]
    step = pl.program_id(0)
    piece = step // (pl.num_programs(0) // PIECES)
    slots = own_ref.shape[1]
    cols = out_ref.shape[0] // 2
    for side, (tab, sources) in enumerate(((own_tab, [own_ref]), (other_tab, other_refs))):
        for col in range(cols):
            slot = jnp.int32(-1)
            for s in range(slots):
                slot = jnp.where(tab[step, s] == col, s, slot)
            block = jnp.zeros(out_ref.shape[1:], BF16)
            for k, ref in enumerate(sources):
                chosen = slot >= 0 if len(sources) == 1 else (slot >= 0) & (piece == k)
                block = jnp.where(chosen, ref[0, jnp.maximum(slot, 0)], block)
            out_ref[side * cols + col] = block


def dense(own_tab, other_tab, own, other, cols):
    steps, slots, tile, _ = own.shape
    depth = steps // PIECES
    tiles = [pl.BlockSpec((1, slots, tile, tile), lambda t: (t, 0, 0, 0))]
    for k in range(PIECES):
        place = lambda t, k=k: (jnp.clip(t - k * depth, 0, depth - 1), 0, 0, 0)
        tiles.append(pl.BlockSpec((1, slots, tile, tile), place))
    return pl.pallas_call(
        dense_kernel,
        grid=(steps,),
        in_specs=[SMEM, SMEM, *tiles],
        out_specs=pl.BlockSpec((2 * cols, tile, tile), lambda t: (0, t, 0)),
        out_shape=jax.ShapeDtypeStruct((2 * cols, steps * tile, tile), BF16),
        compiler_params=params(),
        cost_estimate=pl.CostEstimate(flops=0, bytes_accessed=8 * own.size, transcendentals=0),
    )(own_tab, other_tab, own, *other)


def settle_kernel(code_ref, out_ref):
    copies, rows, width = out_ref.shape
    groups = width // LANES
    units = []
    for k in range(code_ref.shape[0]):
        power = code_ref[k, groups * rows :].astype(jnp.int32).astype(F32)
        power = jnp.concatenate([power[:, :1], power[:, 1:2]], axis=0)
        units.append(jnp.exp2(power - UNIT_BITS))
    for group in range(groups):
        total = None
        for k, unit in enumerate(units):
            code = code_ref[k, group * rows : (group + 1) * rows]
            term = code.astype(jnp.int32).astype(F32) * unit
            total = term if total is None else total + term
        value = total.astype(BF16)
        for k in range(copies):
            out_ref[k, :, group * LANES : (group + 1) * LANES] = value


def settle(codes, part):
    copies, height, _ = codes.shape
    width = height // part * LANES
    return pl.pallas_call(
        settle_kernel,
        in_specs=[VMEM],
        out_specs=VMEM,
        out_shape=jax.ShapeDtypeStruct((copies, part, width), BF16),
        compiler_params=params(),
    )(codes)


def backward_kernel(core_ref, row_ref, factor_ref, out_ref):
    rows, _, part, _ = out_ref.shape
    cols, _, tile = factor_ref.shape
    core = core_ref[0]
    values = row_ref[...].reshape(rows * part, row_ref.shape[2])
    for col in range(cols):
        place = core if col < cols // 2 else 1 - core
        lo = col % (cols // 2) * tile
        block = jnp.dot(values, factor_ref[col], preferred_element_type=F32)
        out_ref[:, place, :, lo : lo + tile] = block.astype(BF16).reshape(rows, part, tile)


def backward(core, rowvals, factor, shape):
    return pl.pallas_call(
        backward_kernel,
        in_specs=[SMEM, VMEM, VMEM],
        out_specs=VMEM,
        out_shape=jax.ShapeDtypeStruct(shape, BF16),
        compiler_params=params(),
        cost_estimate=cost(factor, rowvals.shape[0] * rowvals.shape[1]),
    )(core, rowvals, factor)


def row_sum_kernel(part_ref, out_ref):
    total = part_ref[0].astype(F32)
    for k in range(1, part_ref.shape[0]):
        total = total + part_ref[k].astype(F32)
    out_ref[...] = total


def row_sum(parts):
    return pl.pallas_call(
        row_sum_kernel,
        in_specs=[VMEM],
        out_specs=VMEM,
        out_shape=jax.ShapeDtypeStruct(parts.shape[1:], F32),
        compiler_params=params(),
    )(parts)


def per_device(n_row, n_col, vectors, factor_tiles, tile_columns, live_counts):
    part = vectors.shape[0] // 2
    width = vectors.shape[1]
    col_tiles = width // factor_tiles.shape[2]
    chips = n_col // 2
    pairs = [(c, c ^ 1) for c in range(n_col)]
    same_core = [[core + 2 * p for p in CHIP_ORDERS[core]] for core in range(2)]
    row_core = [
        [r * n_col + 2 * p + core for r in ROW_ORDER for core in range(2)] for p in range(chips)
    ]

    col = lax.axis_index("col")
    core = (col & 1).reshape(1)
    copies = spread(vectors, n_row).reshape(2 * n_row, part, width)
    gathered = swapped(copies, row_core, ("row", "col")).reshape(n_row, 2, part, width)

    slot_index = lax.broadcasted_iota(jnp.int32, tile_columns.shape, 1)
    own_tab = jnp.where(slot_index < live_counts, tile_columns - col * col_tiles, -1)
    other_tab = lax.ppermute(own_tab, "col", pairs)
    other_tiles = []
    for piece in jnp.split(factor_tiles, PIECES):
        piece, other_tab = lax.optimization_barrier((piece, other_tab))
        other_tiles.append(lax.ppermute(piece, "col", pairs))

    factor = dense(own_tab, other_tab, factor_tiles, other_tiles, col_tiles)
    gathered, factor = lax.optimization_barrier((gathered, factor))
    codes = forward(core, own_tab, other_tab, gathered, factor_tiles, other_tiles)
    rowvals = settle(swapped(codes, same_core, "col"), part)
    rowvals = swapped(rowvals, same_core, "col")

    sums = backward(core, rowvals, factor, gathered.shape)
    sums = swapped(sums.reshape(2 * n_row, part, width), row_core, ("row", "col"))
    return row_sum(sums.reshape(n_row, 2 * part, width))


def solution(mesh):
    in_specs = (P("row", "col"), P("row", "col", None, None), P("row", "col"), P("row", "col"))
    body = functools.partial(per_device, mesh.shape["row"], mesh.shape["col"])
    return jax.shard_map(
        body, mesh=mesh, in_specs=in_specs, out_specs=P("row", "col"), check_vma=False
    )
```
